32 devices in a mesh: seq: 8 (over z, x), head: 4 (over y, core).
Axes of the slice: x: 2, y: 2, z: 4, core: 2. Of those that a mesh axis runs over, the one named last changes fastest.
Arguments:
- q_raw: bfloat16 [4096, 2560], P('seq', 'head'), may hold values from -48 to 48
- k_raw: bfloat16 [4096, 2560], P('seq', 'head'), may hold values from -48 to 48
- values: bfloat16 [4096, 2560], P('seq', 'head'), may hold values from -24 to 24
- q_tangent: bfloat16 [4096, 2560], P('seq', 'head'), may hold values from -6 to 6
- k_tangent: bfloat16 [4096, 2560], P('seq', 'head'), may hold values from -6 to 6
- v_tangent: bfloat16 [4096, 2560], P('seq', 'head'), may hold values from -24 to 24
- out_cotangent: bfloat16 [4096, 2560], P('seq', 'head'), may hold values from -24 to 24
- q_gain: float32 [2560], P('head'), may hold values from 0.1 to 1.9
- k_gain: float32 [2560], P('head'), may hold values from 0.1 to 1.9
- tile_at_slot: int32 [32], replicated, may hold values from 0 to 31, as said below
- key_tiles: int32 [32, 6], replicated, may hold values from 0 to 31, as said below
Outputs:
- output: bfloat16 [4096, 2560], P('seq', 'head')
- output_tangent: bfloat16 [4096, 2560], P('seq', 'head')
- grad_q: bfloat16 [4096, 2560], P('seq', 'head')
- grad_k: bfloat16 [4096, 2560], P('seq', 'head')
- grad_v: bfloat16 [4096, 2560], P('seq', 'head')
The draws below stay inside these ranges and needn't reach their ends.
Inputs may be any that keep to these rules, and one draw needn't show every extreme that they name: `tile_at_slot`: a permutation of the tiles. `key_tiles`: row g lists 6 distinct tiles in this order: g itself, 3 other tiles whose slots lie on the same index of seq as g's slot, then 2 tiles whose slots lie on the index just before or just after it. The query tiles of one index of seq name at most 2 distinct tiles of each neighbouring index, and exactly 2 of every neighbour that exists.
All inputs are finite; a program needn't handle non-finite values.
Results may differ from the reference program's by a relative error of at most 0.014.
The reference program's roundings to bfloat16 on the way (of `probs_half`, `prob_tangent` and `score_grad`) count: a program that leaves them out, or rounds other values in their place, can miss the bound.
Values may be sent and summed in bfloat16 or wider, within the bound.
A program may use at most 192 MiB of HBM per device.

```python
import math
import jax
import jax.numpy as jnp
from jax import lax

HEADS = 20
HEAD_DIM = 128
TILE = 128
TPD = 4
NEED = 2
LOCAL_KEYS = 3
REMOTE_KEYS = 2
KSEL = 6
D = 2560
TILES = 32
TOKENS = 4096
N_SEQ = 8


def plan_slots(key):
    devices = TILES // TPD
    perm_key, sets_key, order_key, local_key = jax.random.split(key, 4)
    tile_at_slot = jax.random.permutation(perm_key, TILES).astype(jnp.int32)
    set_keys = jax.random.split(sets_key, devices * 2)
    chosen_sets = jax.vmap(lambda one_key: jax.random.permutation(one_key, TPD)[:NEED])(set_keys).reshape(devices, 2, NEED)
    device_ids = jnp.arange(devices, dtype=jnp.int32)
    neighbour = device_ids[:, None] + jnp.array([-1, 1], jnp.int32)[None, :]
    present = (neighbour >= 0) & (neighbour < devices)
    pool = (neighbour[:, :, None] * TPD + chosen_sets).reshape(devices, 2 * NEED)
    pool_present = jnp.repeat(present, NEED, axis=1)
    order_keys = jax.random.split(order_key, devices)
    ranking = jax.vmap(lambda one_key: jax.random.permutation(one_key, 2 * NEED))(order_keys)
    ranking = ranking + jnp.where(pool_present, 0, 2 * NEED)
    pool_sorted = jnp.take_along_axis(pool, jnp.argsort(ranking, axis=1), axis=1)
    pool_size = jnp.sum(pool_present.astype(jnp.int32), axis=1)
    slot = jnp.arange(TILES, dtype=jnp.int32)
    owner = slot // TPD
    inner = slot % TPD
    picking = inner[:, None] * REMOTE_KEYS + jnp.arange(REMOTE_KEYS, dtype=jnp.int32)[None, :]
    picking = picking % pool_size[owner][:, None]
    remote = jnp.take_along_axis(pool_sorted[owner], picking, axis=1)
    local_keys = jax.random.split(local_key, TILES)
    others = jax.vmap(lambda one_key: jax.random.permutation(one_key, TPD - 1)[:LOCAL_KEYS])(local_keys)
    others = others + (others >= inner[:, None]).astype(jnp.int32)
    nearby = owner[:, None] * TPD + others
    slots = jnp.concatenate([slot[:, None], nearby, remote], axis=1).astype(jnp.int32)
    key_tiles = jnp.zeros((TILES, KSEL), jnp.int32).at[tile_at_slot].set(tile_at_slot[slots])
    return (tile_at_slot, key_tiles)


def draw_tile_at_slot(key, part):
    return plan_slots(key)[0]


def draw_key_tiles(key, part):
    return plan_slots(key)[1]


def draw_q_raw(key, part):
    key = jax.random.fold_in(key, 1)
    noise_key, column_key, row_key = jax.random.split(key, 3)
    columns = jnp.exp(jax.random.uniform(column_key, (D,), minval=math.log(0.2), maxval=math.log(2.0)))
    noise_draw = jax.random.normal(noise_key, (TOKENS, D))
    channel_ramp = jnp.exp(math.log(3.0) * jnp.arange(D) / (D - 1))
    row_scale = jnp.exp(jax.random.uniform(row_key, (TOKENS, 1), minval=math.log(0.2), maxval=math.log(2.0)))
    samples = noise_draw * columns * channel_ramp * row_scale
    return jnp.clip(samples, -48.0, 48.0).astype(jnp.bfloat16)


def draw_k_raw(key, part):
    key = jax.random.fold_in(key, 2)
    noise_key, column_key, row_key = jax.random.split(key, 3)
    columns = jnp.exp(jax.random.uniform(column_key, (D,), minval=math.log(0.2), maxval=math.log(2.0)))
    noise_draw = jax.random.normal(noise_key, (TOKENS, D))
    channel_ramp = jnp.exp(math.log(3.0) * jnp.arange(D) / (D - 1))
    row_scale = jnp.exp(jax.random.uniform(row_key, (TOKENS, 1), minval=math.log(0.2), maxval=math.log(2.0)))
    samples = noise_draw * columns * channel_ramp * row_scale
    return jnp.clip(samples, -48.0, 48.0).astype(jnp.bfloat16)


def levels(stream_key, extent, shards, smallest, high):
    level = 1.0
    for position, shards_of in shards:
        heights = jax.random.uniform(jax.random.fold_in(jax.random.fold_in(stream_key, 6), position), (shards_of,), jnp.float32, smallest / len(shards), high / len(shards))
        level = level * jnp.repeat(jnp.exp(heights), extent[position] // shards_of).reshape((-1,) + (1,) * (len(extent) - 1 - position))
    return level


def centred(stream_key, shape, deviation, bound, shards=(), kind=jnp.bfloat16):
    entries = deviation * jax.random.normal(stream_key, shape, jnp.float32)
    if shards:
        entries = entries * levels(stream_key, shape, shards, -0.22, 0.18)
    return jnp.clip(entries, -bound, bound).astype(kind)


def setup_inputs(seed: int = 0) -> dict:
    key_of = jax.random.split(jax.random.key(seed), 12)
    return {
        "q_raw": draw_q_raw(jax.random.fold_in(key_of[11], 71), 0),
        "k_raw": draw_k_raw(jax.random.fold_in(key_of[11], 71), 0),
        "values": centred(key_of[2], (TOKENS, D), 4.0, 24.0, ((0, 8), (1, 4))),
        "q_tangent": centred(key_of[3], (TOKENS, D), 1.0, 6.0, ((0, 8), (1, 4))),
        "k_tangent": centred(key_of[4], (TOKENS, D), 1.0, 6.0, ((0, 8), (1, 4))),
        "v_tangent": centred(key_of[5], (TOKENS, D), 4.0, 24.0, ((0, 8), (1, 4))),
        "out_cotangent": centred(key_of[6], (TOKENS, D), 4.0, 24.0, ((0, 8), (1, 4))),
        "q_gain": jnp.clip(1.0 + 0.18 * jax.random.normal(key_of[7], (D,), jnp.float32), 0.1, 1.9),
        "k_gain": jnp.clip(1.0 + 0.18 * jax.random.normal(key_of[8], (D,), jnp.float32), 0.1, 1.9),
        "tile_at_slot": draw_tile_at_slot(jax.random.fold_in(key_of[11], 71), 0),
        "key_tiles": draw_key_tiles(jax.random.fold_in(key_of[11], 71), 0),
    }


NORM_EPS = 1e-06
HIGHEST = lax.Precision.HIGHEST

def product(form, left, right):
    return jnp.einsum(form, left.astype(jnp.float32), right.astype(jnp.float32), precision=HIGHEST)

def normalize(raw, tangent, gain):
    raw_float = raw.astype(jnp.float32)
    tangent_float = tangent.astype(jnp.float32)
    inverse = lax.rsqrt(lax.optimization_barrier(jnp.mean(raw_float * raw_float, axis=1, keepdims=True)) + NORM_EPS)
    drift = lax.optimization_barrier(jnp.mean(raw_float * tangent_float, axis=1, keepdims=True))
    normed = (raw_float * inverse * gain).astype(jnp.bfloat16)
    normed_tangent = (gain * (tangent_float * inverse - raw_float * inverse ** 3 * drift)).astype(jnp.bfloat16)
    return (normed, normed_tangent, inverse)

def normalize_back(raw, gain, inverse, incoming):
    raw_float = raw.astype(jnp.float32)
    weighted = gain * incoming
    centre = lax.optimization_barrier(jnp.mean(raw_float * weighted, axis=1, keepdims=True))
    return (inverse * weighted - raw_float * inverse ** 3 * centre).astype(jnp.bfloat16)

def attend(queries, query_tangent, cotangent, keys, key_values, key_tangent, value_tangent, score_scale):
    scores = product('gqhe,gkhe->ghqk', queries, keys) * score_scale
    highest = lax.optimization_barrier(jnp.max(scores, axis=-1, keepdims=True))
    weights = jnp.exp(scores - highest)
    probs = weights / lax.optimization_barrier(jnp.sum(weights, axis=-1, keepdims=True))
    probs_half = probs.astype(jnp.bfloat16)
    output = product('ghqk,gkhe->gqhe', probs_half, key_values).astype(jnp.bfloat16)
    score_tangent = (product('gqhe,gkhe->ghqk', query_tangent, keys) + product('gqhe,gkhe->ghqk', queries, key_tangent)) * score_scale
    centre = lax.optimization_barrier(jnp.sum(probs * score_tangent, axis=-1, keepdims=True))
    prob_tangent = (probs * (score_tangent - centre)).astype(jnp.bfloat16)
    output_tangent = (product('ghqk,gkhe->gqhe', prob_tangent, key_values) + product('ghqk,gkhe->gqhe', probs_half, value_tangent)).astype(jnp.bfloat16)
    prob_grad = product('gqhe,gkhe->ghqk', cotangent, key_values)
    delta = product('gqhe,gqhe->ghq', cotangent, output)
    score_grad = (probs * (prob_grad - delta[..., None])).astype(jnp.bfloat16)
    query_grad = product('ghqk,gkhe->gqhe', score_grad, keys) * score_scale
    key_grad = product('ghqk,gqhe->gkhe', score_grad, queries) * score_scale
    value_grad = product('ghqk,gqhe->gkhe', probs_half, cotangent)
    return (output, output_tangent, query_grad, key_grad, value_grad)

def reference(q_raw, k_raw, values, q_tangent, k_tangent, v_tangent, out_cotangent, q_gain, k_gain, tile_at_slot, key_tiles):
    q_normed, q_normed_tangent, q_inverse = normalize(q_raw, q_tangent, q_gain)
    k_normed, k_normed_tangent, k_inverse = normalize(k_raw, k_tangent, k_gain)
    slot_of = jnp.argsort(tile_at_slot).astype(jnp.int32)
    key_slots = slot_of[key_tiles[tile_at_slot]].astype(jnp.int32)

    def tiled(array):
        return array.reshape(TILES, TILE, HEADS, HEAD_DIM)
    query_tiles = tiled(q_normed)
    query_moving = tiled(q_normed_tangent)
    cotangent_tiles = tiled(out_cotangent)
    key_rows = tiled(k_normed)
    value_rows = tiled(values)
    key_moving = tiled(k_normed_tangent)
    value_moving = tiled(v_tangent)
    score_scale = HEAD_DIM ** (-0.5)
    window = 3 * TPD
    window_range = jnp.arange(window, dtype=jnp.int32)

    def per_device(running, device):
        key_sum, value_sum = running
        start = (device * TPD).astype(jnp.int32)
        indices = lax.dynamic_slice_in_dim(key_slots, start, TPD, 0)

        def picked(array):
            return array[indices.reshape(-1)].reshape(TPD, KSEL * TILE, HEADS, HEAD_DIM)

        def own(array):
            return lax.dynamic_slice_in_dim(array, start, TPD, 0)
        output, output_tangent, query_grad, key_grad, value_grad = attend(own(query_tiles), own(query_moving), own(cotangent_tiles), picked(key_rows), picked(value_rows), picked(key_moving), picked(value_moving), score_scale)
        placing = ((indices - start + TPD)[:, :, None] == window_range[None, None, :]).astype(jnp.float32)
        key_part = product('tkw,tkxc->wxc', placing, key_grad.reshape(TPD, KSEL, TILE, D))
        value_part = product('tkw,tkxc->wxc', placing, value_grad.reshape(TPD, KSEL, TILE, D))
        key_part = lax.optimization_barrier(key_part.astype(jnp.bfloat16)).astype(jnp.float32)
        value_part = lax.optimization_barrier(value_part.astype(jnp.bfloat16)).astype(jnp.float32)
        key_sum = lax.dynamic_update_slice_in_dim(key_sum, lax.dynamic_slice_in_dim(key_sum, start, window, 0) + key_part, start, 0)
        value_sum = lax.dynamic_update_slice_in_dim(value_sum, lax.dynamic_slice_in_dim(value_sum, start, window, 0) + value_part, start, 0)
        return ((key_sum, value_sum), (output, output_tangent, query_grad))
    empty = jnp.zeros((TILES + 2 * TPD, TILE, D), jnp.float32)
    (key_sum, value_sum), (output, output_tangent, query_grad) = lax.scan(per_device, (empty, empty), jnp.arange(N_SEQ, dtype=jnp.int32))
    key_total = key_sum[TPD:TPD + TILES].reshape(TOKENS, D)
    value_total = value_sum[TPD:TPD + TILES].reshape(TOKENS, D)
    grad_q = normalize_back(q_raw, q_gain, q_inverse, query_grad.reshape(TOKENS, D))
    grad_k = normalize_back(k_raw, k_gain, k_inverse, key_total)
    return (output.reshape(TOKENS, D), output_tangent.reshape(TOKENS, D), grad_q, grad_k, value_total.astype(jnp.bfloat16))
```

```python
import functools

import jax
import jax.numpy as jnp
from jax import lax
from jax.experimental import pallas as pl
from jax.experimental.pallas import tpu as pltpu
from jax.sharding import PartitionSpec as P

HEADS = 20
HEAD_DIM = 128
TILE = 128
NEED = 2
KSEL = 6
FULL_WIDTH = HEADS * HEAD_DIM
NORM_EPS = 1e-06
SCALE = HEAD_DIM ** (-0.5)
PACK = NEED * TILE
VMEM_BYTES = 48 * 1024 * 1024
CHUNKS = (2, 2, 1)

VMEM = pl.BlockSpec(memory_space=pltpu.VMEM)
SMEM = pl.BlockSpec(memory_space=pltpu.SMEM)
F32 = jnp.float32
BF16 = jnp.bfloat16


def params():
    return pltpu.CompilerParams(vmem_limit_bytes=VMEM_BYTES)


def shifted(value, axis, steps):
    count = lax.axis_size(axis)
    leading, last = (max(0, -steps), min(count, count - steps))
    return lax.ppermute(value, axis, [(source, source + steps) for source in range(leading, last)])


def chunk_bounds(head_count):
    sizes = CHUNKS if sum(CHUNKS) == head_count else (1,) * head_count
    starts = [sum(sizes[:index]) for index in range(len(sizes))]
    return list(zip(starts, sizes))


def to_rows(columns):
    rows = columns[0].shape[0]
    lane = lax.broadcasted_iota(jnp.int32, (rows, 128), 1)
    packed = jnp.zeros((rows, 128), F32)
    for index, column in enumerate(columns):
        packed = jnp.where(lane == index, column, packed)
    return packed.T[:8]


def to_columns(rows, count):
    padded = jnp.concatenate([rows, jnp.zeros((120, rows.shape[1]), F32)], axis=0).T
    return [padded[:, index : index + 1] for index in range(count)]


def prepare_kernel(
    devices,
    tiles_here,
    position_ref,
    tile_at_slot,
    key_tiles,
    q_ref,
    k_ref,
    qt_ref,
    kt_ref,
    v_ref,
    vt_ref,
    plan_ref,
    up_ref,
    down_ref,
    sums_ref,
    slot_of,
):
    position = position_ref[0]

    def invert(slot, carry):
        slot_of[tile_at_slot[slot]] = slot
        return carry

    lax.fori_loop(0, devices * tiles_here, invert, 0)

    def remote_slots(device):
        return [
            slot_of[key_tiles[tile_at_slot[device * tiles_here + tile], column]]
            for tile in range(tiles_here)
            for column in range(tiles_here, KSEL)
        ]

    def first_last(slots, device):
        first = jnp.int32(tiles_here - 1)
        last = jnp.int32(0)
        for slot in slots:
            offset = slot - device * tiles_here
            inside = (offset >= 0) & (offset < tiles_here)
            first = jnp.where(inside, jnp.minimum(first, offset), first)
            last = jnp.where(inside, jnp.maximum(last, offset), last)
        return first, last

    above = remote_slots(jnp.minimum(position + 1, devices - 1))
    below = remote_slots(jnp.maximum(position - 1, 0))
    here = remote_slots(position)
    up_order = first_last(above, position)
    down_order = first_last(below, position)
    from_below, _ = first_last(here, position - 1)
    from_above, _ = first_last(here, position + 1)
    plan_ref[0], plan_ref[1] = up_order
    plan_ref[2], plan_ref[3] = down_order
    for index, slot in enumerate(here):
        low = jnp.where(slot == (position - 1) * tiles_here + from_below, 0, 1)
        high = jnp.where(slot == (position + 1) * tiles_here + from_above, 2, 3)
        plan_ref[4 + index] = jnp.where(slot < position * tiles_here, low, high)
    for order, packet in ((up_order, up_ref), (down_order, down_ref)):
        for rank in range(NEED):
            source = pl.ds(pl.multiple_of(order[rank] * TILE, TILE), TILE)
            packet[rank * TILE : (rank + 1) * TILE, :] = v_ref[source, :]
            packet[PACK + rank * TILE : PACK + (rank + 1) * TILE, :] = vt_ref[source, :]
    columns = []
    for raw_ref, moving_ref in ((q_ref, qt_ref), (k_ref, kt_ref)):
        raw = raw_ref[...].astype(F32)
        moving = moving_ref[...].astype(F32)
        columns.append(jnp.sum(raw * raw, axis=1, keepdims=True))
        columns.append(jnp.sum(raw * moving, axis=1, keepdims=True))
    sums_ref[...] = to_rows(columns)


def norm_kernel(
    bounds,
    plan,
    totals_ref,
    q_ref,
    k_ref,
    qt_ref,
    kt_ref,
    q_gain_ref,
    k_gain_ref,
    qn_ref,
    qnt_ref,
    kn_ref,
    knt_ref,
    *packets,
):
    totals = to_columns(totals_ref[...], 4)
    for first, raw_ref, moving_ref, gain_ref, normed_ref, tangent_ref in (
        (2, k_ref, kt_ref, k_gain_ref, kn_ref, knt_ref),
        (0, q_ref, qt_ref, q_gain_ref, qn_ref, qnt_ref),
    ):
        inverse = lax.rsqrt(totals[first] / FULL_WIDTH + NORM_EPS)
        drift = totals[first + 1] / FULL_WIDTH
        raw = raw_ref[...].astype(F32)
        moving = moving_ref[...].astype(F32)
        gain = gain_ref[...]
        normed_ref[...] = (raw * inverse * gain).astype(BF16)
        tangent_ref[...] = (
            gain * (moving * inverse - raw * (inverse * inverse * inverse * drift))
        ).astype(BF16)
    for index, (start, size) in enumerate(bounds):
        lanes = slice(start * HEAD_DIM, (start + size) * HEAD_DIM)
        for side in range(2):
            packet = packets[2 * index + side]
            for rank in range(NEED):
                source = pl.ds(pl.multiple_of(plan[2 * side + rank] * TILE, TILE), TILE)
                packet[rank * TILE : (rank + 1) * TILE, :] = kn_ref[source, lanes]
                packet[PACK + rank * TILE : PACK + (rank + 1) * TILE, :] = knt_ref[source, lanes]


def dot(left, right, left_axis, right_axis):
    return lax.dot_general(
        left, right, (((left_axis,), (right_axis,)), ((), ())), preferred_element_type=F32
    )


def attend_kernel(
    tiles_here,
    plan,
    q_ref,
    qt_ref,
    co_ref,
    k_ref,
    kt_ref,
    v_ref,
    vt_ref,
    kb_ref,
    ka_ref,
    vb_ref,
    va_ref,
    out_ref,
    ot_ref,
    qg_ref,
    local_ref,
    below_ref,
    above_ref,
    remote,
    remote_sum,
    local_sum,
):
    rows = tiles_here * TILE
    for base, kp_ref, vp_ref in ((0, kb_ref, vb_ref), (PACK, ka_ref, va_ref)):
        remote[base : base + PACK, 0:128] = kp_ref[:PACK, :]
        remote[base : base + PACK, 128:256] = kp_ref[PACK:, :]
        remote[base : base + PACK, 256:384] = vp_ref[:PACK, :]
        remote[base : base + PACK, 384:512] = vp_ref[PACK:, :]
    remote_sum[...] = jnp.zeros_like(remote_sum)
    k_local = jnp.concatenate([k_ref[...], kt_ref[...]], axis=1)
    v_local = jnp.concatenate([v_ref[...], vt_ref[...]], axis=1)
    for tile in range(tiles_here):
        here = slice(tile * TILE, (tile + 1) * TILE)
        places = [
            pl.ds(pl.multiple_of(plan[4 + tile * 2 + column] * TILE, TILE), TILE)
            for column in range(2)
        ]
        keys = jnp.concatenate([k_local] + [remote[place, 0:256] for place in places], axis=0)
        vals = jnp.concatenate([v_local] + [remote[place, 256:512] for place in places], axis=0)
        query, moving, cotangent = q_ref[here, :], qt_ref[here, :], co_ref[here, :]
        scores = dot(query, keys[:, :128], 1, 1)
        highest = jnp.max(scores, axis=1, keepdims=True)
        weights = jnp.exp((scores - highest) * SCALE)
        probs = weights * (1.0 / jnp.sum(weights, axis=1, keepdims=True))
        probs_half = probs.astype(BF16)
        both = dot(probs_half, vals, 1, 0)
        output = both[:, :128].astype(BF16)
        out_ref[here, :] = output
        score_tangent = dot(jnp.concatenate([moving, query], axis=1), keys, 1, 1) * SCALE
        centre = jnp.sum(probs * score_tangent, axis=1, keepdims=True)
        prob_tangent = (probs * (score_tangent - centre)).astype(BF16)
        ot_ref[here, :] = (dot(prob_tangent, vals[:, :128], 1, 0) + both[:, 128:]).astype(BF16)
        prob_grad = dot(cotangent, vals[:, :128], 1, 1)
        delta = jnp.sum(cotangent.astype(F32) * output.astype(F32), axis=1, keepdims=True)
        score_grad = (probs * (prob_grad - delta)).astype(BF16)
        qg_ref[here, :] = dot(score_grad, keys[:, :128], 1, 0) * SCALE
        key_grad = dot(score_grad, query, 0, 0)
        value_grad = dot(probs_half, cotangent, 0, 0)
        if tile == 0:
            local_sum[:, :128] = key_grad[:rows]
            local_sum[:, 128:] = value_grad[:rows]
        else:
            local_sum[:, :128] += key_grad[:rows]
            local_sum[:, 128:] += value_grad[:rows]
        for column, place in enumerate(places):
            piece = slice(rows + column * TILE, rows + (column + 1) * TILE)
            remote_sum[place, :128] += key_grad[piece]
            remote_sum[place, 128:] += value_grad[piece]
    local_ref[:rows, :] = (local_sum[:, :128] * SCALE).astype(BF16)
    local_ref[rows:, :] = local_sum[:, 128:].astype(BF16)
    for base, part_ref in ((0, below_ref), (PACK, above_ref)):
        part_ref[:PACK, :] = (remote_sum[base : base + PACK, :128] * SCALE).astype(BF16)
        part_ref[PACK:, :] = remote_sum[base : base + PACK, 128:].astype(BF16)


def merge_kernel(bounds, plan, q_ref, k_ref, q_gain_ref, k_gain_ref, *refs):
    count = len(bounds)
    qg, local, from_above, from_below = (refs[index * count : (index + 1) * count] for index in range(4))
    grad_v_ref, key_ref, sums_ref, value_ref = refs[4 * count :]
    rows = q_ref.shape[0]
    q_sum = jnp.zeros((rows, 1), F32)
    for index, (start, size) in enumerate(bounds):
        lanes = slice(start * HEAD_DIM, (start + size) * HEAD_DIM)
        key_ref[:, lanes] = local[index][:rows, :].astype(F32)
        value_ref[:, lanes] = local[index][rows:, :].astype(F32)
        for side, returned in enumerate((from_above[index], from_below[index])):
            for rank in range(NEED):
                place = pl.ds(pl.multiple_of(plan[2 * side + rank] * TILE, TILE), TILE)
                piece = slice(rank * TILE, (rank + 1) * TILE)
                key_ref[place, lanes] += returned[piece, :].astype(F32)
                piece = slice(PACK + rank * TILE, PACK + (rank + 1) * TILE)
                value_ref[place, lanes] += returned[piece, :].astype(F32)
        q_sum += jnp.sum(
            q_ref[:, lanes].astype(F32) * (q_gain_ref[:, lanes] * qg[index][...]),
            axis=1,
            keepdims=True,
        )
    grad_v_ref[...] = value_ref[...].astype(BF16)
    k_sum = jnp.sum(
        k_ref[...].astype(F32) * (k_gain_ref[...] * key_ref[...]), axis=1, keepdims=True
    )
    sums_ref[...] = to_rows([q_sum, k_sum])


def final_kernel(
    bounds, totals_ref, back_ref, q_ref, k_ref, q_gain_ref, k_gain_ref, key_ref, *refs
):
    count = len(bounds)
    qg, (grad_q_ref, grad_k_ref) = refs[:count], refs[count:]
    totals = to_columns(totals_ref[...], 4)
    back = to_columns(back_ref[...], 2)
    q_inverse = lax.rsqrt(totals[0] / FULL_WIDTH + NORM_EPS)
    k_inverse = lax.rsqrt(totals[2] / FULL_WIDTH + NORM_EPS)
    q_pull = q_inverse * q_inverse * q_inverse * (back[0] / FULL_WIDTH)
    k_pull = k_inverse * k_inverse * k_inverse * (back[1] / FULL_WIDTH)
    for index, (start, size) in enumerate(bounds):
        lanes = slice(start * HEAD_DIM, (start + size) * HEAD_DIM)
        grad_q_ref[:, lanes] = (
            q_inverse * (q_gain_ref[:, lanes] * qg[index][...])
            - q_ref[:, lanes].astype(F32) * q_pull
        ).astype(BF16)
    grad_k_ref[...] = (
        k_inverse * (k_gain_ref[...] * key_ref[...]) - k_ref[...].astype(F32) * k_pull
    ).astype(BF16)


def per_device(
    q_raw,
    k_raw,
    values,
    q_tangent,
    k_tangent,
    v_tangent,
    out_cotangent,
    q_gain,
    k_gain,
    tile_at_slot,
    key_tiles,
):
    rows, width = q_raw.shape
    head_count = width // HEAD_DIM
    tiles_here = rows // TILE
    devices = lax.axis_size("seq")
    bounds = chunk_bounds(head_count)
    position = lax.axis_index("seq").astype(jnp.int32).reshape(1)
    q_gain = q_gain.reshape(1, width)
    k_gain = k_gain.reshape(1, width)
    struct = jax.ShapeDtypeStruct

    plan, v_up, v_down, sums = pl.pallas_call(
        functools.partial(prepare_kernel, devices, tiles_here),
        out_shape=[
            struct((16,), jnp.int32),
            struct((2 * PACK, width), BF16),
            struct((2 * PACK, width), BF16),
            struct((8, rows), F32),
        ],
        in_specs=[SMEM] * 3 + [VMEM] * 6,
        out_specs=[SMEM] + [VMEM] * 3,
        scratch_shapes=[pltpu.SMEM((devices * tiles_here,), jnp.int32)],
        compiler_params=params(),
        name="prepare",
    )(position, tile_at_slot, key_tiles, q_raw, k_raw, q_tangent, k_tangent, values, v_tangent)
    v_below = shifted(v_up, "seq", 1)
    v_above = shifted(v_down, "seq", -1)
    totals = lax.psum(sums, "head")
    packet_shapes = [
        struct((2 * PACK, size * HEAD_DIM), BF16) for _, size in bounds for _ in range(2)
    ]
    qn, qnt, kn, knt, *packets = pl.pallas_call(
        functools.partial(norm_kernel, bounds),
        out_shape=[struct((rows, width), BF16)] * 4 + packet_shapes,
        in_specs=[SMEM] + [VMEM] * 7,
        out_specs=[VMEM] * (4 + len(packet_shapes)),
        compiler_params=params(),
        name="norm",
    )(plan, totals, q_raw, k_raw, q_tangent, k_tangent, q_gain, k_gain)
    k_below = [shifted(packet, "seq", 1) for packet in packets[0::2]]
    k_above = [shifted(packet, "seq", -1) for packet in packets[1::2]]

    results = []
    for index, (start, size) in enumerate(bounds):
        def whole(head, plan_ref, start=start):
            return (0, start + head)

        def part(head, plan_ref):
            return (0, head)

        full_spec = pl.BlockSpec((rows, HEAD_DIM), whole)
        results.append(
            pl.pallas_call(
                functools.partial(attend_kernel, tiles_here),
                grid_spec=pltpu.PrefetchScalarGridSpec(
                    num_scalar_prefetch=1,
                    grid=(size,),
                    in_specs=[full_spec] * 7
                    + [pl.BlockSpec((2 * PACK, HEAD_DIM), part)] * 2
                    + [pl.BlockSpec((2 * PACK, HEAD_DIM), whole)] * 2,
                    out_specs=[pl.BlockSpec((rows, HEAD_DIM), part)] * 3
                    + [pl.BlockSpec((2 * rows, HEAD_DIM), part)]
                    + [pl.BlockSpec((2 * PACK, HEAD_DIM), part)] * 2,
                    scratch_shapes=[
                        pltpu.VMEM((2 * PACK, 4 * HEAD_DIM), BF16),
                        pltpu.VMEM((2 * PACK, 2 * HEAD_DIM), F32),
                        pltpu.VMEM((rows, 2 * HEAD_DIM), F32),
                    ],
                ),
                out_shape=[
                    struct((rows, size * HEAD_DIM), BF16),
                    struct((rows, size * HEAD_DIM), BF16),
                    struct((rows, size * HEAD_DIM), F32),
                    struct((2 * rows, size * HEAD_DIM), BF16),
                    struct((2 * PACK, size * HEAD_DIM), BF16),
                    struct((2 * PACK, size * HEAD_DIM), BF16),
                ],
                cost_estimate=pl.CostEstimate(
                    flops=20 * size * rows * KSEL * TILE * HEAD_DIM,
                    bytes_accessed=24 * size * rows * HEAD_DIM,
                    transcendentals=size * rows * KSEL * TILE,
                ),
                compiler_params=params(),
                name="attend",
            )(
                plan, qn, qnt, out_cotangent, kn, knt, values, v_tangent,
                k_below[index], k_above[index], v_below, v_above,
            )
        )
    outs, tangents, query_grads, locals_, to_below, to_above = zip(*results)
    from_above = [shifted(packet, "seq", -1) for packet in to_below]
    from_below = [shifted(packet, "seq", 1) for packet in to_above]
    count = len(bounds)
    grad_v, key_total, back_sums = pl.pallas_call(
        functools.partial(merge_kernel, bounds),
        out_shape=[
            struct((rows, width), BF16), struct((rows, width), F32), struct((8, rows), F32)
        ],
        in_specs=[SMEM] + [VMEM] * (4 + 4 * count),
        out_specs=[VMEM] * 3,
        scratch_shapes=[pltpu.VMEM((rows, width), F32)],
        compiler_params=params(),
        name="merge",
    )(plan, q_raw, k_raw, q_gain, k_gain, *query_grads, *locals_, *from_above, *from_below)
    back = lax.psum(back_sums, "head")
    grad_q, grad_k = pl.pallas_call(
        functools.partial(final_kernel, bounds),
        out_shape=[struct((rows, width), BF16)] * 2,
        in_specs=[VMEM] * (7 + count),
        out_specs=[VMEM] * 2,
        compiler_params=params(),
        name="final",
    )(totals, back, q_raw, k_raw, q_gain, k_gain, key_total, *query_grads)
    return (
        jnp.concatenate(outs, axis=1),
        jnp.concatenate(tangents, axis=1),
        grad_q,
        grad_k,
        grad_v,
    )


def solution(mesh):
    rows, lanes, copied = P("seq", "head"), P("head"), P()
    return jax.shard_map(
        per_device,
        mesh=mesh,
        in_specs=(rows,) * 7 + (lanes,) * 2 + (copied,) * 2,
        out_specs=(rows,) * 5,
        check_vma=False,
    )
```

```python
import functools

import jax
import jax.numpy as jnp
from jax import lax
from jax.experimental import pallas as pl
from jax.experimental.pallas import tpu as pltpu
from jax.sharding import PartitionSpec as P

HEADS = 20
HEAD_DIM = 128
TILE = 128
NEED = 2
KSEL = 6
FULL_WIDTH = HEADS * HEAD_DIM
NORM_EPS = 1e-06
SCALE = HEAD_DIM ** (-0.5)
PACK = NEED * TILE
VMEM_BYTES = 48 * 1024 * 1024
CHUNKS = (2, 2, 1)

VMEM = pl.BlockSpec(memory_space=pltpu.VMEM)
SMEM = pl.BlockSpec(memory_space=pltpu.SMEM)
HBM = pl.BlockSpec(memory_space=pltpu.HBM)
F32 = jnp.float32
BF16 = jnp.bfloat16


def params():
    return pltpu.CompilerParams(vmem_limit_bytes=VMEM_BYTES)


def shifted(value, axis, steps):
    count = lax.axis_size(axis)
    leading, last = (max(0, -steps), min(count, count - steps))
    return lax.ppermute(value, axis, [(source, source + steps) for source in range(leading, last)])


def chunk_bounds(head_count):
    sizes = CHUNKS if sum(CHUNKS) == head_count else (1,) * head_count
    starts = [sum(sizes[:index]) for index in range(len(sizes))]
    return list(zip(starts, sizes))


def to_rows(columns):
    rows = columns[0].shape[0]
    lane = lax.broadcasted_iota(jnp.int32, (rows, 128), 1)
    packed = jnp.zeros((rows, 128), F32)
    for index, column in enumerate(columns):
        packed = jnp.where(lane == index, column, packed)
    return packed.T[:8]


def to_columns(rows, count):
    padded = jnp.concatenate([rows, jnp.zeros((120, rows.shape[1]), F32)], axis=0).T
    return [padded[:, index : index + 1] for index in range(count)]


def prepare_kernel(
    devices,
    tiles_here,
    position_ref,
    tile_at_slot,
    key_tiles,
    v_ref,
    vt_ref,
    plan_ref,
    up_ref,
    down_ref,
    slot_of,
    copy_sem,
):
    position = position_ref[0]

    def invert(slot, carry):
        slot_of[tile_at_slot[slot]] = slot
        return carry

    lax.fori_loop(0, devices * tiles_here, invert, 0)

    def remote_slots(device):
        return [
            slot_of[key_tiles[tile_at_slot[device * tiles_here + tile], column]]
            for tile in range(tiles_here)
            for column in range(tiles_here, KSEL)
        ]

    def first_last(slots, device):
        first = jnp.int32(tiles_here - 1)
        last = jnp.int32(0)
        for slot in slots:
            offset = slot - device * tiles_here
            inside = (offset >= 0) & (offset < tiles_here)
            first = jnp.where(inside, jnp.minimum(first, offset), first)
            last = jnp.where(inside, jnp.maximum(last, offset), last)
        return first, last

    above = remote_slots(jnp.minimum(position + 1, devices - 1))
    below = remote_slots(jnp.maximum(position - 1, 0))
    here = remote_slots(position)
    up_order = first_last(above, position)
    down_order = first_last(below, position)
    from_below, _ = first_last(here, position - 1)
    from_above, _ = first_last(here, position + 1)
    plan_ref[0], plan_ref[1] = up_order
    plan_ref[2], plan_ref[3] = down_order
    for index, slot in enumerate(here):
        low = jnp.where(slot == (position - 1) * tiles_here + from_below, 0, 1)
        high = jnp.where(slot == (position + 1) * tiles_here + from_above, 2, 3)
        plan_ref[4 + index] = jnp.where(slot < position * tiles_here, low, high)
    copies = []
    for order, packet in ((up_order, up_ref), (down_order, down_ref)):
        for rank in range(NEED):
            source = pl.ds(pl.multiple_of(order[rank] * TILE, TILE), TILE)
            for base, array_ref in ((0, v_ref), (PACK, vt_ref)):
                copies.append(
                    pltpu.make_async_copy(
                        array_ref.at[source, :],
                        packet.at[pl.ds(base + rank * TILE, TILE), :],
                        copy_sem.at[len(copies)],
                    )
                )
    for copy in copies:
        copy.start()
    for copy in copies:
        copy.wait()


def sums_kernel(q_ref, k_ref, qt_ref, kt_ref, sums_ref):
    columns = []
    for raw_ref, moving_ref in ((q_ref, qt_ref), (k_ref, kt_ref)):
        raw = raw_ref[...].astype(F32)
        moving = moving_ref[...].astype(F32)
        columns.append(jnp.sum(raw * raw, axis=1, keepdims=True))
        columns.append(jnp.sum(raw * moving, axis=1, keepdims=True))
    sums_ref[...] = to_rows(columns)


def exchange_kernel(count, part_ref, total_ref, arrived, send_sem, recv_sem):
    me = lax.axis_index("head")
    barrier = pltpu.get_barrier_semaphore()
    for step in range(1, count):
        pl.semaphore_signal(
            barrier,
            inc=1,
            device_id={"head": lax.rem(me + step, count)},
            device_id_type=pl.DeviceIdType.MESH,
        )
    pl.semaphore_wait(barrier, count - 1)
    copies = [
        pltpu.make_async_remote_copy(
            src_ref=part_ref,
            dst_ref=arrived.at[step - 1],
            send_sem=send_sem.at[step - 1],
            recv_sem=recv_sem.at[step - 1],
            device_id={"head": lax.rem(me + step, count)},
            device_id_type=pl.DeviceIdType.MESH,
        )
        for step in range(1, count)
    ]
    for copy in copies:
        copy.start()
    for copy in copies:
        copy.wait()
    total = part_ref[...]
    for step in range(1, count):
        total += arrived[step - 1]
    total_ref[...] = total


def head_total(part, collective_id):
    count = lax.axis_size("head")
    return pl.pallas_call(
        functools.partial(exchange_kernel, count),
        out_shape=jax.ShapeDtypeStruct(part.shape, F32),
        in_specs=[VMEM],
        out_specs=VMEM,
        scratch_shapes=[
            pltpu.VMEM((count - 1,) + part.shape, F32),
            pltpu.SemaphoreType.DMA((count - 1,)),
            pltpu.SemaphoreType.DMA((count - 1,)),
        ],
        compiler_params=pltpu.CompilerParams(
            collective_id=collective_id, has_side_effects=True
        ),
        name="exchange",
    )(part)


def norm_kernel(
    bounds,
    plan,
    totals_ref,
    q_ref,
    k_ref,
    qt_ref,
    kt_ref,
    q_gain_ref,
    k_gain_ref,
    qn_ref,
    qnt_ref,
    kn_ref,
    knt_ref,
    *packets,
):
    totals = to_columns(totals_ref[...], 4)
    for first, raw_ref, moving_ref, gain_ref, normed_ref, tangent_ref in (
        (2, k_ref, kt_ref, k_gain_ref, kn_ref, knt_ref),
        (0, q_ref, qt_ref, q_gain_ref, qn_ref, qnt_ref),
    ):
        inverse = lax.rsqrt(totals[first] / FULL_WIDTH + NORM_EPS)
        drift = totals[first + 1] / FULL_WIDTH
        raw = raw_ref[...].astype(F32)
        moving = moving_ref[...].astype(F32)
        gain = gain_ref[...]
        normed_ref[...] = (raw * inverse * gain).astype(BF16)
        tangent_ref[...] = (
            gain * (moving * inverse - raw * (inverse * inverse * inverse * drift))
        ).astype(BF16)
    for index, (start, size) in enumerate(bounds):
        lanes = slice(start * HEAD_DIM, (start + size) * HEAD_DIM)
        for side in range(2):
            packet = packets[2 * index + side]
            for rank in range(NEED):
                source = pl.ds(pl.multiple_of(plan[2 * side + rank] * TILE, TILE), TILE)
                packet[rank * TILE : (rank + 1) * TILE, :] = kn_ref[source, lanes]
                packet[PACK + rank * TILE : PACK + (rank + 1) * TILE, :] = knt_ref[source, lanes]


def dot(left, right, left_axis, right_axis):
    return lax.dot_general(
        left, right, (((left_axis,), (right_axis,)), ((), ())), preferred_element_type=F32
    )


def attend_kernel(
    tiles_here,
    plan,
    q_ref,
    qt_ref,
    co_ref,
    k_ref,
    kt_ref,
    v_ref,
    vt_ref,
    kb_ref,
    ka_ref,
    vb_ref,
    va_ref,
    out_ref,
    ot_ref,
    qg_ref,
    local_ref,
    below_ref,
    above_ref,
    remote,
    remote_sum,
    local_sum,
):
    rows = tiles_here * TILE
    for base, kp_ref, vp_ref in ((0, kb_ref, vb_ref), (PACK, ka_ref, va_ref)):
        remote[base : base + PACK, 0:128] = kp_ref[:PACK, :]
        remote[base : base + PACK, 128:256] = kp_ref[PACK:, :]
        remote[base : base + PACK, 256:384] = vp_ref[:PACK, :]
        remote[base : base + PACK, 384:512] = vp_ref[PACK:, :]
    remote_sum[...] = jnp.zeros_like(remote_sum)
    k_local = jnp.concatenate([k_ref[...], kt_ref[...]], axis=1)
    v_local = jnp.concatenate([v_ref[...], vt_ref[...]], axis=1)
    for tile in range(tiles_here):
        here = slice(tile * TILE, (tile + 1) * TILE)
        places = [
            pl.ds(pl.multiple_of(plan[4 + tile * 2 + column] * TILE, TILE), TILE)
            for column in range(2)
        ]
        keys = jnp.concatenate([k_local] + [remote[place, 0:256] for place in places], axis=0)
        vals = jnp.concatenate([v_local] + [remote[place, 256:512] for place in places], axis=0)
        query, moving, cotangent = q_ref[here, :], qt_ref[here, :], co_ref[here, :]
        scores = dot(query, keys[:, :128], 1, 1)
        highest = jnp.max(scores, axis=1, keepdims=True)
        weights = jnp.exp((scores - highest) * SCALE)
        probs = weights * (1.0 / jnp.sum(weights, axis=1, keepdims=True))
        probs_half = probs.astype(BF16)
        both = dot(probs_half, vals, 1, 0)
        output = both[:, :128].astype(BF16)
        out_ref[here, :] = output
        score_tangent = dot(jnp.concatenate([moving, query], axis=1), keys, 1, 1) * SCALE
        centre = jnp.sum(probs * score_tangent, axis=1, keepdims=True)
        prob_tangent = (probs * (score_tangent - centre)).astype(BF16)
        ot_ref[here, :] = (dot(prob_tangent, vals[:, :128], 1, 0) + both[:, 128:]).astype(BF16)
        prob_grad = dot(cotangent, vals[:, :128], 1, 1)
        delta = jnp.sum(cotangent.astype(F32) * output.astype(F32), axis=1, keepdims=True)
        score_grad = (probs * (prob_grad - delta)).astype(BF16)
        qg_ref[here, :] = dot(score_grad, keys[:, :128], 1, 0) * SCALE
        key_grad = dot(score_grad, query, 0, 0)
        value_grad = dot(probs_half, cotangent, 0, 0)
        if tile == 0:
            local_sum[:, :128] = key_grad[:rows]
            local_sum[:, 128:] = value_grad[:rows]
        else:
            local_sum[:, :128] += key_grad[:rows]
            local_sum[:, 128:] += value_grad[:rows]
        for column, place in enumerate(places):
            piece = slice(rows + column * TILE, rows + (column + 1) * TILE)
            remote_sum[place, :128] += key_grad[piece]
            remote_sum[place, 128:] += value_grad[piece]
    local_ref[:rows, :] = (local_sum[:, :128] * SCALE).astype(BF16)
    local_ref[rows:, :] = local_sum[:, 128:].astype(BF16)
    for base, part_ref in ((0, below_ref), (PACK, above_ref)):
        part_ref[:PACK, :] = (remote_sum[base : base + PACK, :128] * SCALE).astype(BF16)
        part_ref[PACK:, :] = remote_sum[base : base + PACK, 128:].astype(BF16)


def merge_kernel(bounds, plan, q_ref, k_ref, q_gain_ref, k_gain_ref, *refs):
    count = len(bounds)
    qg, local, from_above, from_below = (refs[index * count : (index + 1) * count] for index in range(4))
    grad_v_ref, key_ref, sums_ref, value_ref = refs[4 * count :]
    rows = q_ref.shape[0]
    q_sum = jnp.zeros((rows, 1), F32)
    for index, (start, size) in enumerate(bounds):
        lanes = slice(start * HEAD_DIM, (start + size) * HEAD_DIM)
        key_ref[:, lanes] = local[index][:rows, :].astype(F32)
        value_ref[:, lanes] = local[index][rows:, :].astype(F32)
        for side, returned in enumerate((from_above[index], from_below[index])):
            for rank in range(NEED):
                place = pl.ds(pl.multiple_of(plan[2 * side + rank] * TILE, TILE), TILE)
                piece = slice(rank * TILE, (rank + 1) * TILE)
                key_ref[place, lanes] += returned[piece, :].astype(F32)
                piece = slice(PACK + rank * TILE, PACK + (rank + 1) * TILE)
                value_ref[place, lanes] += returned[piece, :].astype(F32)
        q_sum += jnp.sum(
            q_ref[:, lanes].astype(F32) * (q_gain_ref[:, lanes] * qg[index][...]),
            axis=1,
            keepdims=True,
        )
    grad_v_ref[...] = value_ref[...].astype(BF16)
    k_sum = jnp.sum(
        k_ref[...].astype(F32) * (k_gain_ref[...] * key_ref[...]), axis=1, keepdims=True
    )
    sums_ref[...] = to_rows([q_sum, k_sum])


def final_kernel(
    bounds, totals_ref, back_ref, q_ref, k_ref, q_gain_ref, k_gain_ref, key_ref, *refs
):
    count = len(bounds)
    qg, (grad_q_ref, grad_k_ref) = refs[:count], refs[count:]
    totals = to_columns(totals_ref[...], 4)
    back = to_columns(back_ref[...], 2)
    q_inverse = lax.rsqrt(totals[0] / FULL_WIDTH + NORM_EPS)
    k_inverse = lax.rsqrt(totals[2] / FULL_WIDTH + NORM_EPS)
    q_pull = q_inverse * q_inverse * q_inverse * (back[0] / FULL_WIDTH)
    k_pull = k_inverse * k_inverse * k_inverse * (back[1] / FULL_WIDTH)
    for index, (start, size) in enumerate(bounds):
        lanes = slice(start * HEAD_DIM, (start + size) * HEAD_DIM)
        grad_q_ref[:, lanes] = (
            q_inverse * (q_gain_ref[:, lanes] * qg[index][...])
            - q_ref[:, lanes].astype(F32) * q_pull
        ).astype(BF16)
    grad_k_ref[...] = (
        k_inverse * (k_gain_ref[...] * key_ref[...]) - k_ref[...].astype(F32) * k_pull
    ).astype(BF16)


def per_device(
    q_raw,
    k_raw,
    values,
    q_tangent,
    k_tangent,
    v_tangent,
    out_cotangent,
    q_gain,
    k_gain,
    tile_at_slot,
    key_tiles,
):
    rows, width = q_raw.shape
    head_count = width // HEAD_DIM
    tiles_here = rows // TILE
    devices = lax.axis_size("seq")
    bounds = chunk_bounds(head_count)
    position = lax.axis_index("seq").astype(jnp.int32).reshape(1)
    q_gain = q_gain.reshape(1, width)
    k_gain = k_gain.reshape(1, width)
    struct = jax.ShapeDtypeStruct

    plan, v_up, v_down = pl.pallas_call(
        functools.partial(prepare_kernel, devices, tiles_here),
        out_shape=[
            struct((16,), jnp.int32),
            struct((2 * PACK, width), BF16),
            struct((2 * PACK, width), BF16),
        ],
        in_specs=[SMEM] * 3 + [HBM] * 2,
        out_specs=[SMEM] + [HBM] * 2,
        scratch_shapes=[
            pltpu.SMEM((devices * tiles_here,), jnp.int32),
            pltpu.SemaphoreType.DMA((4 * NEED,)),
        ],
        compiler_params=params(),
        name="prepare",
    )(position, tile_at_slot, key_tiles, values, v_tangent)
    v_below = shifted(v_up, "seq", 1)
    v_above = shifted(v_down, "seq", -1)
    sums = pl.pallas_call(
        sums_kernel,
        out_shape=struct((8, rows), F32),
        in_specs=[VMEM] * 4,
        out_specs=VMEM,
        compiler_params=params(),
        name="sums",
    )(q_raw, k_raw, q_tangent, k_tangent)
    totals = head_total(sums, 0)
    packet_shapes = [
        struct((2 * PACK, size * HEAD_DIM), BF16) for _, size in bounds for _ in range(2)
    ]
    qn, qnt, kn, knt, *packets = pl.pallas_call(
        functools.partial(norm_kernel, bounds),
        out_shape=[struct((rows, width), BF16)] * 4 + packet_shapes,
        in_specs=[SMEM] + [VMEM] * 7,
        out_specs=[VMEM] * (4 + len(packet_shapes)),
        compiler_params=params(),
        name="norm",
    )(plan, totals, q_raw, k_raw, q_tangent, k_tangent, q_gain, k_gain)
    k_below = [shifted(packet, "seq", 1) for packet in packets[0::2]]
    k_above = [shifted(packet, "seq", -1) for packet in packets[1::2]]

    results = []
    for index, (start, size) in enumerate(bounds):
        def whole(head, plan_ref, start=start):
            return (0, start + head)

        def part(head, plan_ref):
            return (0, head)

        full_spec = pl.BlockSpec((rows, HEAD_DIM), whole)
        results.append(
            pl.pallas_call(
                functools.partial(attend_kernel, tiles_here),
                grid_spec=pltpu.PrefetchScalarGridSpec(
                    num_scalar_prefetch=1,
                    grid=(size,),
                    in_specs=[full_spec] * 7
                    + [pl.BlockSpec((2 * PACK, HEAD_DIM), part)] * 2
                    + [pl.BlockSpec((2 * PACK, HEAD_DIM), whole)] * 2,
                    out_specs=[pl.BlockSpec((rows, HEAD_DIM), part)] * 3
                    + [pl.BlockSpec((2 * rows, HEAD_DIM), part)]
                    + [pl.BlockSpec((2 * PACK, HEAD_DIM), part)] * 2,
                    scratch_shapes=[
                        pltpu.VMEM((2 * PACK, 4 * HEAD_DIM), BF16),
                        pltpu.VMEM((2 * PACK, 2 * HEAD_DIM), F32),
                        pltpu.VMEM((rows, 2 * HEAD_DIM), F32),
                    ],
                ),
                out_shape=[
                    struct((rows, size * HEAD_DIM), BF16),
                    struct((rows, size * HEAD_DIM), BF16),
                    struct((rows, size * HEAD_DIM), F32),
                    struct((2 * rows, size * HEAD_DIM), BF16),
                    struct((2 * PACK, size * HEAD_DIM), BF16),
                    struct((2 * PACK, size * HEAD_DIM), BF16),
                ],
                cost_estimate=pl.CostEstimate(
                    flops=20 * size * rows * KSEL * TILE * HEAD_DIM,
                    bytes_accessed=24 * size * rows * HEAD_DIM,
                    transcendentals=size * rows * KSEL * TILE,
                ),
                compiler_params=params(),
                name="attend",
            )(
                plan, qn, qnt, out_cotangent, kn, knt, values, v_tangent,
                k_below[index], k_above[index], v_below, v_above,
            )
        )
    outs, tangents, query_grads, locals_, to_below, to_above = zip(*results)
    from_above = [shifted(packet, "seq", -1) for packet in to_below]
    from_below = [shifted(packet, "seq", 1) for packet in to_above]
    count = len(bounds)
    grad_v, key_total, back_sums = pl.pallas_call(
        functools.partial(merge_kernel, bounds),
        out_shape=[
            struct((rows, width), BF16), struct((rows, width), F32), struct((8, rows), F32)
        ],
        in_specs=[SMEM] + [VMEM] * (4 + 4 * count),
        out_specs=[VMEM] * 3,
        scratch_shapes=[pltpu.VMEM((rows, width), F32)],
        compiler_params=params(),
        name="merge",
    )(plan, q_raw, k_raw, q_gain, k_gain, *query_grads, *locals_, *from_above, *from_below)
    back = head_total(back_sums, 1)
    grad_q, grad_k = pl.pallas_call(
        functools.partial(final_kernel, bounds),
        out_shape=[struct((rows, width), BF16)] * 2,
        in_specs=[VMEM] * (7 + count),
        out_specs=[VMEM] * 2,
        compiler_params=params(),
        name="final",
    )(totals, back, q_raw, k_raw, q_gain, k_gain, key_total, *query_grads)
    return (
        jnp.concatenate(outs, axis=1),
        jnp.concatenate(tangents, axis=1),
        grad_q,
        grad_k,
        grad_v,
    )


def solution(mesh):
    rows, lanes, copied = P("seq", "head"), P("head"), P()
    return jax.shard_map(
        per_device,
        mesh=mesh,
        in_specs=(rows,) * 7 + (lanes,) * 2 + (copied,) * 2,
        out_specs=(rows,) * 5,
        check_vma=False,
    )
```

```python
import functools

import jax
import jax.numpy as jnp
from jax import lax
from jax.experimental import pallas as pl
from jax.experimental.pallas import tpu as pltpu
from jax.sharding import PartitionSpec as P

HEADS = 20
HEAD_DIM = 128
TILE = 128
NEED = 2
KSEL = 6
FULL_WIDTH = HEADS * HEAD_DIM
NORM_EPS = 1e-06
SCALE = HEAD_DIM ** (-0.5)
PACK = NEED * TILE
VMEM_BYTES = 48 * 1024 * 1024
CHUNKS = (3, 2)

VMEM = pl.BlockSpec(memory_space=pltpu.VMEM)
SMEM = pl.BlockSpec(memory_space=pltpu.SMEM)
HBM = pl.BlockSpec(memory_space=pltpu.HBM)
F32 = jnp.float32
BF16 = jnp.bfloat16


def params():
    return pltpu.CompilerParams(vmem_limit_bytes=VMEM_BYTES)


def shifted(value, axis, steps):
    count = lax.axis_size(axis)
    leading, last = (max(0, -steps), min(count, count - steps))
    return lax.ppermute(value, axis, [(source, source + steps) for source in range(leading, last)])


def chunk_bounds(head_count):
    sizes = CHUNKS if sum(CHUNKS) == head_count else (1,) * head_count
    starts = [sum(sizes[:index]) for index in range(len(sizes))]
    return list(zip(starts, sizes))


def to_rows(columns):
    rows = columns[0].shape[0]
    lane = lax.broadcasted_iota(jnp.int32, (rows, 128), 1)
    packed = jnp.zeros((rows, 128), F32)
    for index, column in enumerate(columns):
        packed = jnp.where(lane == index, column, packed)
    return packed.T[:8]


def to_columns(rows, count):
    padded = jnp.concatenate([rows, jnp.zeros((120, rows.shape[1]), F32)], axis=0).T
    return [padded[:, index : index + 1] for index in range(count)]


def prepare_kernel(
    devices,
    tiles_here,
    position_ref,
    tile_at_slot,
    key_tiles,
    v_ref,
    vt_ref,
    plan_ref,
    up_ref,
    down_ref,
    slot_of,
    copy_sem,
):
    position = position_ref[0]

    def invert(slot, carry):
        slot_of[tile_at_slot[slot]] = slot
        return carry

    lax.fori_loop(0, devices * tiles_here, invert, 0)

    def remote_slots(device):
        return [
            slot_of[key_tiles[tile_at_slot[device * tiles_here + tile], column]]
            for tile in range(tiles_here)
            for column in range(tiles_here, KSEL)
        ]

    def first_last(slots, device):
        first = jnp.int32(tiles_here - 1)
        last = jnp.int32(0)
        for slot in slots:
            offset = slot - device * tiles_here
            inside = (offset >= 0) & (offset < tiles_here)
            first = jnp.where(inside, jnp.minimum(first, offset), first)
            last = jnp.where(inside, jnp.maximum(last, offset), last)
        return first, last

    above = remote_slots(jnp.minimum(position + 1, devices - 1))
    below = remote_slots(jnp.maximum(position - 1, 0))
    here = remote_slots(position)
    up_order = first_last(above, position)
    down_order = first_last(below, position)
    from_below, _ = first_last(here, position - 1)
    from_above, _ = first_last(here, position + 1)
    plan_ref[0], plan_ref[1] = up_order
    plan_ref[2], plan_ref[3] = down_order
    for index, slot in enumerate(here):
        low = jnp.where(slot == (position - 1) * tiles_here + from_below, 0, 1)
        high = jnp.where(slot == (position + 1) * tiles_here + from_above, 2, 3)
        plan_ref[4 + index] = jnp.where(slot < position * tiles_here, low, high)
    copies = []
    for order, packet in ((up_order, up_ref), (down_order, down_ref)):
        for rank in range(NEED):
            source = pl.ds(pl.multiple_of(order[rank] * TILE, TILE), TILE)
            for base, array_ref in ((0, v_ref), (PACK, vt_ref)):
                copies.append(
                    pltpu.make_async_copy(
                        array_ref.at[source, :],
                        packet.at[pl.ds(base + rank * TILE, TILE), :],
                        copy_sem.at[len(copies)],
                    )
                )
    for copy in copies:
        copy.start()
    for copy in copies:
        copy.wait()


def sums_kernel(q_ref, k_ref, qt_ref, kt_ref, sums_ref):
    columns = []
    for raw_ref, moving_ref in ((q_ref, qt_ref), (k_ref, kt_ref)):
        raw = raw_ref[...].astype(F32)
        moving = moving_ref[...].astype(F32)
        columns.append(jnp.sum(raw * raw, axis=1, keepdims=True))
        columns.append(jnp.sum(raw * moving, axis=1, keepdims=True))
    sums_ref[...] = to_rows(columns)


def exchange_kernel(count, part_ref, total_ref, arrived, send_sem, recv_sem):
    me = lax.axis_index("head")
    barrier = pltpu.get_barrier_semaphore()
    for step in range(1, count):
        pl.semaphore_signal(
            barrier,
            inc=1,
            device_id={"head": lax.rem(me + step, count)},
            device_id_type=pl.DeviceIdType.MESH,
        )
    pl.semaphore_wait(barrier, count - 1)
    copies = [
        pltpu.make_async_remote_copy(
            src_ref=part_ref,
            dst_ref=arrived.at[step - 1],
            send_sem=send_sem.at[step - 1],
            recv_sem=recv_sem.at[step - 1],
            device_id={"head": lax.rem(me + step, count)},
            device_id_type=pl.DeviceIdType.MESH,
        )
        for step in range(1, count)
    ]
    for copy in copies:
        copy.start()
    for copy in copies:
        copy.wait()
    total = part_ref[...]
    for step in range(1, count):
        total += arrived[step - 1]
    total_ref[...] = total


def head_total(part, collective_id):
    count = lax.axis_size("head")
    return pl.pallas_call(
        functools.partial(exchange_kernel, count),
        out_shape=jax.ShapeDtypeStruct(part.shape, F32),
        in_specs=[VMEM],
        out_specs=VMEM,
        scratch_shapes=[
            pltpu.VMEM((count - 1,) + part.shape, F32),
            pltpu.SemaphoreType.DMA((count - 1,)),
            pltpu.SemaphoreType.DMA((count - 1,)),
        ],
        compiler_params=pltpu.CompilerParams(
            collective_id=collective_id, has_side_effects=True
        ),
        name="exchange",
    )(part)


def norm_kernel(
    bounds,
    plan,
    totals_ref,
    q_ref,
    k_ref,
    qt_ref,
    kt_ref,
    q_gain_ref,
    k_gain_ref,
    qn_ref,
    qnt_ref,
    kn_ref,
    knt_ref,
    *packets,
):
    totals = to_columns(totals_ref[...], 4)
    for first, raw_ref, moving_ref, gain_ref, normed_ref, tangent_ref in (
        (2, k_ref, kt_ref, k_gain_ref, kn_ref, knt_ref),
        (0, q_ref, qt_ref, q_gain_ref, qn_ref, qnt_ref),
    ):
        inverse = lax.rsqrt(totals[first] / FULL_WIDTH + NORM_EPS)
        drift = totals[first + 1] / FULL_WIDTH
        raw = raw_ref[...].astype(F32)
        moving = moving_ref[...].astype(F32)
        gain = gain_ref[...]
        normed_ref[...] = (raw * inverse * gain).astype(BF16)
        tangent_ref[...] = (
            gain * (moving * inverse - raw * (inverse * inverse * inverse * drift))
        ).astype(BF16)
    for index, (start, size) in enumerate(bounds):
        lanes = slice(start * HEAD_DIM, (start + size) * HEAD_DIM)
        for side in range(2):
            packet = packets[2 * index + side]
            for rank in range(NEED):
                source = pl.ds(pl.multiple_of(plan[2 * side + rank] * TILE, TILE), TILE)
                packet[rank * TILE : (rank + 1) * TILE, :] = kn_ref[source, lanes]
                packet[PACK + rank * TILE : PACK + (rank + 1) * TILE, :] = knt_ref[source, lanes]


def dot(left, right, left_axis, right_axis):
    return lax.dot_general(
        left, right, (((left_axis,), (right_axis,)), ((), ())), preferred_element_type=F32
    )


def attend_kernel(
    tiles_here,
    plan,
    q_ref,
    qt_ref,
    co_ref,
    k_ref,
    kt_ref,
    v_ref,
    vt_ref,
    kb_ref,
    ka_ref,
    vb_ref,
    va_ref,
    out_ref,
    ot_ref,
    qg_ref,
    local_ref,
    below_ref,
    above_ref,
    remote,
    remote_sum,
    prob_buf,
    tangent_buf,
    grad_buf,
    probs_half,
    prob_tangent,
    score_grad,
):
    rows = tiles_here * TILE
    for base, kp_ref, vp_ref in ((0, kb_ref, vb_ref), (PACK, ka_ref, va_ref)):
        remote[base : base + PACK, 0:128] = kp_ref[:PACK, :]
        remote[base : base + PACK, 128:256] = kp_ref[PACK:, :]
        remote[base : base + PACK, 256:384] = vp_ref[:PACK, :]
        remote[base : base + PACK, 384:512] = vp_ref[PACK:, :]
    remote_sum[...] = jnp.zeros_like(remote_sum)
    tiles = [slice(tile * TILE, (tile + 1) * TILE) for tile in range(tiles_here)]
    places = [
        [
            pl.ds(pl.multiple_of(plan[4 + tile * 2 + column] * TILE, TILE), TILE)
            for column in range(2)
        ]
        for tile in range(tiles_here)
    ]

    def far(tile, start, stop):
        return jnp.concatenate([remote[place, start:stop] for place in places[tile]], axis=0)

    k_local = jnp.concatenate([k_ref[...], kt_ref[...]], axis=1)
    v_local = jnp.concatenate([v_ref[...], vt_ref[...]], axis=1)
    query, cotangent = q_ref[...], co_ref[...]
    moving = jnp.concatenate([qt_ref[...], query], axis=1)
    prob_buf[:, :rows] = dot(query, k_ref[...], 1, 1)
    tangent_buf[:, :rows] = dot(moving, k_local, 1, 1)
    grad_buf[:, :rows] = dot(cotangent, v_ref[...], 1, 1)
    for tile, here in enumerate(tiles):
        prob_buf[here, rows:] = dot(query[here], far(tile, 0, 128), 1, 1)
        tangent_buf[here, rows:] = dot(moving[here], far(tile, 0, 256), 1, 1)
        grad_buf[here, rows:] = dot(cotangent[here], far(tile, 256, 384), 1, 1)
    for here in tiles:
        scores = prob_buf[here, :]
        highest = jnp.max(scores, axis=1, keepdims=True)
        weights = jnp.exp((scores - highest) * SCALE)
        probs = weights * (1.0 / jnp.sum(weights, axis=1, keepdims=True))
        prob_buf[here, :] = probs
        probs_half[here, :] = probs.astype(BF16)
        score_tangent = tangent_buf[here, :] * SCALE
        centre = jnp.sum(probs * score_tangent, axis=1, keepdims=True)
        prob_tangent[here, :] = (probs * (score_tangent - centre)).astype(BF16)
    both = dot(probs_half[:, :rows], v_local, 1, 0)
    moved = dot(prob_tangent[:, :rows], v_ref[...], 1, 0)
    for tile, here in enumerate(tiles):
        pair = both[here] + dot(probs_half[here, rows:], far(tile, 256, 512), 1, 0)
        output = pair[:, :128].astype(BF16)
        out_ref[here, :] = output
        ot_ref[here, :] = (
            moved[here] + dot(prob_tangent[here, rows:], far(tile, 256, 384), 1, 0) + pair[:, 128:]
        ).astype(BF16)
        delta = jnp.sum(cotangent[here].astype(F32) * output.astype(F32), axis=1, keepdims=True)
        score_grad[here, :] = (prob_buf[here, :] * (grad_buf[here, :] - delta)).astype(BF16)
    near = dot(score_grad[:, :rows], k_ref[...], 1, 0)
    for tile, here in enumerate(tiles):
        qg_ref[here, :] = (near[here] + dot(score_grad[here, rows:], far(tile, 0, 128), 1, 0)) * SCALE
        key_grad = dot(score_grad[here, rows:], query[here], 0, 0)
        value_grad = dot(probs_half[here, rows:], cotangent[here], 0, 0)
        for column, place in enumerate(places[tile]):
            piece = slice(column * TILE, (column + 1) * TILE)
            remote_sum[place, :128] += key_grad[piece]
            remote_sum[place, 128:] += value_grad[piece]
    local_ref[:rows, :] = (dot(score_grad[:, :rows], query, 0, 0) * SCALE).astype(BF16)
    local_ref[rows:, :] = dot(probs_half[:, :rows], cotangent, 0, 0).astype(BF16)
    for base, part_ref in ((0, below_ref), (PACK, above_ref)):
        part_ref[:PACK, :] = (remote_sum[base : base + PACK, :128] * SCALE).astype(BF16)
        part_ref[PACK:, :] = remote_sum[base : base + PACK, 128:].astype(BF16)


def merge_kernel(bounds, plan, q_ref, k_ref, q_gain_ref, k_gain_ref, *refs):
    count = len(bounds)
    qg, local, from_above, from_below = (refs[index * count : (index + 1) * count] for index in range(4))
    grad_v_ref, key_ref, sums_ref, value_ref = refs[4 * count :]
    rows = q_ref.shape[0]
    q_sum = jnp.zeros((rows, 1), F32)
    for index, (start, size) in enumerate(bounds):
        lanes = slice(start * HEAD_DIM, (start + size) * HEAD_DIM)
        key_ref[:, lanes] = local[index][:rows, :].astype(F32)
        value_ref[:, lanes] = local[index][rows:, :].astype(F32)
        for side, returned in enumerate((from_above[index], from_below[index])):
            for rank in range(NEED):
                place = pl.ds(pl.multiple_of(plan[2 * side + rank] * TILE, TILE), TILE)
                piece = slice(rank * TILE, (rank + 1) * TILE)
                key_ref[place, lanes] += returned[piece, :].astype(F32)
                piece = slice(PACK + rank * TILE, PACK + (rank + 1) * TILE)
                value_ref[place, lanes] += returned[piece, :].astype(F32)
        q_sum += jnp.sum(
            q_ref[:, lanes].astype(F32) * (q_gain_ref[:, lanes] * qg[index][...]),
            axis=1,
            keepdims=True,
        )
    grad_v_ref[...] = value_ref[...].astype(BF16)
    k_sum = jnp.sum(
        k_ref[...].astype(F32) * (k_gain_ref[...] * key_ref[...]), axis=1, keepdims=True
    )
    sums_ref[...] = to_rows([q_sum, k_sum])


def final_kernel(
    bounds, totals_ref, back_ref, q_ref, k_ref, q_gain_ref, k_gain_ref, key_ref, *refs
):
    count = len(bounds)
    qg, (grad_q_ref, grad_k_ref) = refs[:count], refs[count:]
    totals = to_columns(totals_ref[...], 4)
    back = to_columns(back_ref[...], 2)
    q_inverse = lax.rsqrt(totals[0] / FULL_WIDTH + NORM_EPS)
    k_inverse = lax.rsqrt(totals[2] / FULL_WIDTH + NORM_EPS)
    q_pull = q_inverse * q_inverse * q_inverse * (back[0] / FULL_WIDTH)
    k_pull = k_inverse * k_inverse * k_inverse * (back[1] / FULL_WIDTH)
    for index, (start, size) in enumerate(bounds):
        lanes = slice(start * HEAD_DIM, (start + size) * HEAD_DIM)
        grad_q_ref[:, lanes] = (
            q_inverse * (q_gain_ref[:, lanes] * qg[index][...])
            - q_ref[:, lanes].astype(F32) * q_pull
        ).astype(BF16)
    grad_k_ref[...] = (
        k_inverse * (k_gain_ref[...] * key_ref[...]) - k_ref[...].astype(F32) * k_pull
    ).astype(BF16)


def per_device(
    q_raw,
    k_raw,
    values,
    q_tangent,
    k_tangent,
    v_tangent,
    out_cotangent,
    q_gain,
    k_gain,
    tile_at_slot,
    key_tiles,
):
    rows, width = q_raw.shape
    head_count = width // HEAD_DIM
    tiles_here = rows // TILE
    devices = lax.axis_size("seq")
    bounds = chunk_bounds(head_count)
    position = lax.axis_index("seq").astype(jnp.int32).reshape(1)
    q_gain = q_gain.reshape(1, width)
    k_gain = k_gain.reshape(1, width)
    struct = jax.ShapeDtypeStruct

    plan, v_up, v_down = pl.pallas_call(
        functools.partial(prepare_kernel, devices, tiles_here),
        out_shape=[
            struct((16,), jnp.int32),
            struct((2 * PACK, width), BF16),
            struct((2 * PACK, width), BF16),
        ],
        in_specs=[SMEM] * 3 + [HBM] * 2,
        out_specs=[SMEM] + [HBM] * 2,
        scratch_shapes=[
            pltpu.SMEM((devices * tiles_here,), jnp.int32),
            pltpu.SemaphoreType.DMA((4 * NEED,)),
        ],
        compiler_params=params(),
        name="prepare",
    )(position, tile_at_slot, key_tiles, values, v_tangent)
    v_below = shifted(v_up, "seq", 1)
    v_above = shifted(v_down, "seq", -1)
    sums = pl.pallas_call(
        sums_kernel,
        out_shape=struct((8, rows), F32),
        in_specs=[VMEM] * 4,
        out_specs=VMEM,
        compiler_params=params(),
        name="sums",
    )(q_raw, k_raw, q_tangent, k_tangent)
    totals = head_total(sums, 0)
    packet_shapes = [
        struct((2 * PACK, size * HEAD_DIM), BF16) for _, size in bounds for _ in range(2)
    ]
    qn, qnt, kn, knt, *packets = pl.pallas_call(
        functools.partial(norm_kernel, bounds),
        out_shape=[struct((rows, width), BF16)] * 4 + packet_shapes,
        in_specs=[SMEM] + [VMEM] * 7,
        out_specs=[VMEM] * (4 + len(packet_shapes)),
        compiler_params=params(),
        name="norm",
    )(plan, totals, q_raw, k_raw, q_tangent, k_tangent, q_gain, k_gain)
    k_below = [shifted(packet, "seq", 1) for packet in packets[0::2]]
    k_above = [shifted(packet, "seq", -1) for packet in packets[1::2]]

    results = []
    for index, (start, size) in enumerate(bounds):
        def whole(head, plan_ref, start=start):
            return (0, start + head)

        def part(head, plan_ref):
            return (0, head)

        full_spec = pl.BlockSpec((rows, HEAD_DIM), whole)
        results.append(
            pl.pallas_call(
                functools.partial(attend_kernel, tiles_here),
                grid_spec=pltpu.PrefetchScalarGridSpec(
                    num_scalar_prefetch=1,
                    grid=(size,),
                    in_specs=[full_spec] * 7
                    + [pl.BlockSpec((2 * PACK, HEAD_DIM), part)] * 2
                    + [pl.BlockSpec((2 * PACK, HEAD_DIM), whole)] * 2,
                    out_specs=[pl.BlockSpec((rows, HEAD_DIM), part)] * 3
                    + [pl.BlockSpec((2 * rows, HEAD_DIM), part)]
                    + [pl.BlockSpec((2 * PACK, HEAD_DIM), part)] * 2,
                    scratch_shapes=[
                        pltpu.VMEM((2 * PACK, 4 * HEAD_DIM), BF16),
                        pltpu.VMEM((2 * PACK, 2 * HEAD_DIM), F32),
                    ]
                    + [pltpu.VMEM((rows, KSEL * TILE), F32)] * 3
                    + [pltpu.VMEM((rows, KSEL * TILE), BF16)] * 3,
                ),
                out_shape=[
                    struct((rows, size * HEAD_DIM), BF16),
                    struct((rows, size * HEAD_DIM), BF16),
                    struct((rows, size * HEAD_DIM), F32),
                    struct((2 * rows, size * HEAD_DIM), BF16),
                    struct((2 * PACK, size * HEAD_DIM), BF16),
                    struct((2 * PACK, size * HEAD_DIM), BF16),
                ],
                cost_estimate=pl.CostEstimate(
                    flops=20 * size * rows * KSEL * TILE * HEAD_DIM,
                    bytes_accessed=24 * size * rows * HEAD_DIM,
                    transcendentals=size * rows * KSEL * TILE,
                ),
                compiler_params=params(),
                name="attend",
            )(
                plan, qn, qnt, out_cotangent, kn, knt, values, v_tangent,
                k_below[index], k_above[index], v_below, v_above,
            )
        )
    outs, tangents, query_grads, locals_, to_below, to_above = zip(*results)
    from_above = [shifted(packet, "seq", -1) for packet in to_below]
    from_below = [shifted(packet, "seq", 1) for packet in to_above]
    count = len(bounds)
    grad_v, key_total, back_sums = pl.pallas_call(
        functools.partial(merge_kernel, bounds),
        out_shape=[
            struct((rows, width), BF16), struct((rows, width), F32), struct((8, rows), F32)
        ],
        in_specs=[SMEM] + [VMEM] * (4 + 4 * count),
        out_specs=[VMEM] * 3,
        scratch_shapes=[pltpu.VMEM((rows, width), F32)],
        compiler_params=params(),
        name="merge",
    )(plan, q_raw, k_raw, q_gain, k_gain, *query_grads, *locals_, *from_above, *from_below)
    back = head_total(back_sums, 1)
    grad_q, grad_k = pl.pallas_call(
        functools.partial(final_kernel, bounds),
        out_shape=[struct((rows, width), BF16)] * 2,
        in_specs=[VMEM] * (7 + count),
        out_specs=[VMEM] * 2,
        compiler_params=params(),
        name="final",
    )(totals, back, q_raw, k_raw, q_gain, k_gain, key_total, *query_grads)
    return (
        jnp.concatenate(outs, axis=1),
        jnp.concatenate(tangents, axis=1),
        grad_q,
        grad_k,
        grad_v,
    )


def solution(mesh):
    rows, lanes, copied = P("seq", "head"), P("head"), P()
    return jax.shard_map(
        per_device,
        mesh=mesh,
        in_specs=(rows,) * 7 + (lanes,) * 2 + (copied,) * 2,
        out_specs=(rows,) * 5,
        check_vma=False,
    )
```

```python
import functools

import jax
import jax.numpy as jnp
from jax import lax
from jax.experimental import pallas as pl
from jax.experimental.pallas import tpu as pltpu
from jax.sharding import PartitionSpec as P

HEADS = 20
HEAD_DIM = 128
TILE = 128
NEED = 2
KSEL = 6
FULL_WIDTH = HEADS * HEAD_DIM
NORM_EPS = 1e-06
SCALE = HEAD_DIM ** (-0.5)
PACK = NEED * TILE
VMEM_BYTES = 24 * 1024 * 1024
CHUNKS = (2, 3)

VMEM = pl.BlockSpec(memory_space=pltpu.VMEM)
SMEM = pl.BlockSpec(memory_space=pltpu.SMEM)
HBM = pl.BlockSpec(memory_space=pl.ANY)
F32 = jnp.float32
BF16 = jnp.bfloat16


def params():
    return pltpu.CompilerParams(vmem_limit_bytes=VMEM_BYTES)


def shifted(value, axis, steps):
    count = lax.axis_size(axis)
    leading, last = (max(0, -steps), min(count, count - steps))
    return lax.ppermute(value, axis, [(source, source + steps) for source in range(leading, last)])


def chunk_bounds(head_count):
    sizes = CHUNKS if sum(CHUNKS) == head_count else (1,) * head_count
    starts = [sum(sizes[:index]) for index in range(len(sizes))]
    return list(zip(starts, sizes))


def to_rows(columns):
    rows = columns[0].shape[0]
    lane = lax.broadcasted_iota(jnp.int32, (rows, 128), 1)
    packed = jnp.zeros((rows, 128), F32)
    for index, column in enumerate(columns):
        packed = jnp.where(lane == index, column, packed)
    return packed.T[:8]


def to_columns(rows, count):
    padded = jnp.concatenate([rows, jnp.zeros((120, rows.shape[1]), F32)], axis=0).T
    return [padded[:, index : index + 1] for index in range(count)]


def prepare_kernel(
    devices,
    tiles_here,
    position_ref,
    tile_at_slot,
    key_tiles,
    v_ref,
    vt_ref,
    plan_ref,
    up_ref,
    down_ref,
    slot_of,
    copy_sem,
):
    position = position_ref[0]

    def invert(slot, carry):
        slot_of[tile_at_slot[slot]] = slot
        return carry

    lax.fori_loop(0, devices * tiles_here, invert, 0)

    def remote_slots(device):
        return [
            slot_of[key_tiles[tile_at_slot[device * tiles_here + tile], column]]
            for tile in range(tiles_here)
            for column in range(tiles_here, KSEL)
        ]

    def first_last(slots, device):
        first = jnp.int32(tiles_here - 1)
        last = jnp.int32(0)
        for slot in slots:
            offset = slot - device * tiles_here
            inside = (offset >= 0) & (offset < tiles_here)
            first = jnp.where(inside, jnp.minimum(first, offset), first)
            last = jnp.where(inside, jnp.maximum(last, offset), last)
        return first, last

    above = remote_slots(jnp.minimum(position + 1, devices - 1))
    below = remote_slots(jnp.maximum(position - 1, 0))
    here = remote_slots(position)
    up_order = first_last(above, position)
    down_order = first_last(below, position)
    from_below, _ = first_last(here, position - 1)
    from_above, _ = first_last(here, position + 1)
    plan_ref[0], plan_ref[1] = up_order
    plan_ref[2], plan_ref[3] = down_order
    for index, slot in enumerate(here):
        low = jnp.where(slot == (position - 1) * tiles_here + from_below, 0, 1)
        high = jnp.where(slot == (position + 1) * tiles_here + from_above, 2, 3)
        plan_ref[4 + index] = jnp.where(slot < position * tiles_here, low, high)
    copies = []
    for order, packet in ((up_order, up_ref), (down_order, down_ref)):
        for rank in range(NEED):
            source = pl.ds(pl.multiple_of(order[rank] * TILE, TILE), TILE)
            for base, array_ref in ((0, v_ref), (PACK, vt_ref)):
                copies.append(
                    pltpu.make_async_copy(
                        array_ref.at[source, :],
                        packet.at[pl.ds(base + rank * TILE, TILE), :],
                        copy_sem.at[len(copies)],
                    )
                )
    for copy in copies:
        copy.start()
    for copy in copies:
        copy.wait()


def sums_kernel(q_ref, k_ref, qt_ref, kt_ref, sums_ref):
    columns = []
    for raw_ref, moving_ref in ((q_ref, qt_ref), (k_ref, kt_ref)):
        raw = raw_ref[...].astype(F32)
        moving = moving_ref[...].astype(F32)
        columns.append(jnp.sum(raw * raw, axis=1, keepdims=True))
        columns.append(jnp.sum(raw * moving, axis=1, keepdims=True))
    sums_ref[...] = to_rows(columns)


def exchange_kernel(count, part_ref, total_ref, arrived, send_sem, recv_sem):
    me = lax.axis_index("head")
    barrier = pltpu.get_barrier_semaphore()
    for step in range(1, count):
        pl.semaphore_signal(
            barrier,
            inc=1,
            device_id={"head": lax.rem(me + step, count)},
            device_id_type=pl.DeviceIdType.MESH,
        )
    pl.semaphore_wait(barrier, count - 1)
    copies = [
        pltpu.make_async_remote_copy(
            src_ref=part_ref,
            dst_ref=arrived.at[step - 1],
            send_sem=send_sem.at[step - 1],
            recv_sem=recv_sem.at[step - 1],
            device_id={"head": lax.rem(me + step, count)},
            device_id_type=pl.DeviceIdType.MESH,
        )
        for step in range(1, count)
    ]
    for copy in copies:
        copy.start()
    for copy in copies:
        copy.wait()
    total = part_ref[...]
    for step in range(1, count):
        total += arrived[step - 1]
    total_ref[...] = total


def head_total(part, collective_id):
    count = lax.axis_size("head")
    return pl.pallas_call(
        functools.partial(exchange_kernel, count),
        out_shape=jax.ShapeDtypeStruct(part.shape, F32),
        in_specs=[VMEM],
        out_specs=VMEM,
        scratch_shapes=[
            pltpu.VMEM((count - 1,) + part.shape, F32),
            pltpu.SemaphoreType.DMA((count - 1,)),
            pltpu.SemaphoreType.DMA((count - 1,)),
        ],
        compiler_params=pltpu.CompilerParams(
            collective_id=collective_id,
            has_side_effects=True,
            vmem_limit_bytes=2 * 1024 * 1024,
        ),
        name="exchange",
    )(part)


def norm_kernel(
    bounds,
    plan,
    totals_ref,
    q_ref,
    k_ref,
    qt_ref,
    kt_ref,
    q_gain_ref,
    k_gain_ref,
    qn_ref,
    qnt_ref,
    kn_ref,
    knt_ref,
    *packets,
):
    totals = to_columns(totals_ref[...], 4)
    for first, raw_ref, moving_ref, gain_ref, normed_ref, tangent_ref in (
        (2, k_ref, kt_ref, k_gain_ref, kn_ref, knt_ref),
        (0, q_ref, qt_ref, q_gain_ref, qn_ref, qnt_ref),
    ):
        inverse = lax.rsqrt(totals[first] / FULL_WIDTH + NORM_EPS)
        drift = totals[first + 1] / FULL_WIDTH
        raw = raw_ref[...].astype(F32)
        moving = moving_ref[...].astype(F32)
        gain = gain_ref[...]
        normed_ref[...] = (raw * inverse * gain).astype(BF16)
        tangent_ref[...] = (
            gain * (moving * inverse - raw * (inverse * inverse * inverse * drift))
        ).astype(BF16)
    for index, (start, size) in enumerate(bounds):
        lanes = slice(start * HEAD_DIM, (start + size) * HEAD_DIM)
        for side in range(2):
            packet = packets[2 * index + side]
            for rank in range(NEED):
                source = pl.ds(pl.multiple_of(plan[2 * side + rank] * TILE, TILE), TILE)
                packet[rank * TILE : (rank + 1) * TILE, :] = kn_ref[source, lanes]
                packet[PACK + rank * TILE : PACK + (rank + 1) * TILE, :] = knt_ref[source, lanes]


def dot(left, right, left_axis, right_axis):
    return lax.dot_general(
        left, right, (((left_axis,), (right_axis,)), ((), ())), preferred_element_type=F32
    )


def attend_kernel(
    tiles_here,
    plan,
    q_ref,
    qt_ref,
    co_ref,
    k_ref,
    kt_ref,
    v_ref,
    vt_ref,
    kb_ref,
    ka_ref,
    vb_ref,
    va_ref,
    out_ref,
    ot_ref,
    qg_ref,
    local_ref,
    below_ref,
    above_ref,
    remote,
    remote_sum,
    prob_buf,
    tangent_buf,
    grad_buf,
    probs_half,
    prob_tangent,
    score_grad,
):
    rows = tiles_here * TILE
    for base, kp_ref, vp_ref in ((0, kb_ref, vb_ref), (PACK, ka_ref, va_ref)):
        remote[base : base + PACK, 0:128] = kp_ref[:PACK, :]
        remote[base : base + PACK, 128:256] = kp_ref[PACK:, :]
        remote[base : base + PACK, 256:384] = vp_ref[:PACK, :]
        remote[base : base + PACK, 384:512] = vp_ref[PACK:, :]
    remote_sum[...] = jnp.zeros_like(remote_sum)
    tiles = [slice(tile * TILE, (tile + 1) * TILE) for tile in range(tiles_here)]
    places = [
        [
            pl.ds(pl.multiple_of(plan[4 + tile * 2 + column] * TILE, TILE), TILE)
            for column in range(2)
        ]
        for tile in range(tiles_here)
    ]

    def far(tile, start, stop):
        return jnp.concatenate([remote[place, start:stop] for place in places[tile]], axis=0)

    k_local = jnp.concatenate([k_ref[...], kt_ref[...]], axis=1)
    v_local = jnp.concatenate([v_ref[...], vt_ref[...]], axis=1)
    query, cotangent = q_ref[...], co_ref[...]
    moving = jnp.concatenate([qt_ref[...], query], axis=1)
    prob_buf[:, :rows] = dot(query, k_ref[...], 1, 1)
    tangent_buf[:, :rows] = dot(moving, k_local, 1, 1)
    grad_buf[:, :rows] = dot(cotangent, v_ref[...], 1, 1)
    for tile, here in enumerate(tiles):
        prob_buf[here, rows:] = dot(query[here], far(tile, 0, 128), 1, 1)
        tangent_buf[here, rows:] = dot(moving[here], far(tile, 0, 256), 1, 1)
        grad_buf[here, rows:] = dot(cotangent[here], far(tile, 256, 384), 1, 1)
    for here in tiles:
        scores = prob_buf[here, :]
        highest = jnp.max(scores, axis=1, keepdims=True)
        weights = jnp.exp((scores - highest) * SCALE)
        probs = weights * (1.0 / jnp.sum(weights, axis=1, keepdims=True))
        prob_buf[here, :] = probs
        probs_half[here, :] = probs.astype(BF16)
        score_tangent = tangent_buf[here, :] * SCALE
        centre = jnp.sum(probs * score_tangent, axis=1, keepdims=True)
        prob_tangent[here, :] = (probs * (score_tangent - centre)).astype(BF16)
    both = dot(probs_half[:, :rows], v_local, 1, 0)
    moved = dot(prob_tangent[:, :rows], v_ref[...], 1, 0)
    for tile, here in enumerate(tiles):
        pair = both[here] + dot(probs_half[here, rows:], far(tile, 256, 512), 1, 0)
        output = pair[:, :128].astype(BF16)
        out_ref[here, :] = output
        ot_ref[here, :] = (
            moved[here] + dot(prob_tangent[here, rows:], far(tile, 256, 384), 1, 0) + pair[:, 128:]
        ).astype(BF16)
        delta = jnp.sum(cotangent[here].astype(F32) * output.astype(F32), axis=1, keepdims=True)
        score_grad[here, :] = (prob_buf[here, :] * (grad_buf[here, :] - delta)).astype(BF16)
    near = dot(score_grad[:, :rows], k_ref[...], 1, 0)
    for tile, here in enumerate(tiles):
        qg_ref[here, :] = (near[here] + dot(score_grad[here, rows:], far(tile, 0, 128), 1, 0)) * SCALE
        key_grad = dot(score_grad[here, rows:], query[here], 0, 0)
        value_grad = dot(probs_half[here, rows:], cotangent[here], 0, 0)
        for column, place in enumerate(places[tile]):
            piece = slice(column * TILE, (column + 1) * TILE)
            remote_sum[place, :128] += key_grad[piece]
            remote_sum[place, 128:] += value_grad[piece]
    local_ref[:rows, :] = (dot(score_grad[:, :rows], query, 0, 0) * SCALE).astype(BF16)
    local_ref[rows:, :] = dot(probs_half[:, :rows], cotangent, 0, 0).astype(BF16)
    for base, part_ref in ((0, below_ref), (PACK, above_ref)):
        part_ref[:PACK, :] = (remote_sum[base : base + PACK, :128] * SCALE).astype(BF16)
        part_ref[PACK:, :] = remote_sum[base : base + PACK, 128:].astype(BF16)


def merge_kernel(bounds, plan, q_ref, k_ref, q_gain_ref, k_gain_ref, *refs):
    count = len(bounds)
    qg, local, from_above, from_below = (refs[index * count : (index + 1) * count] for index in range(4))
    grad_v_ref, key_ref, sums_ref, value_ref = refs[4 * count :]
    rows = q_ref.shape[0]
    q_sum = jnp.zeros((rows, 1), F32)
    for index, (start, size) in enumerate(bounds):
        lanes = slice(start * HEAD_DIM, (start + size) * HEAD_DIM)
        key_ref[:, lanes] = local[index][:rows, :].astype(F32)
        value_ref[:, lanes] = local[index][rows:, :].astype(F32)
        for side, returned in enumerate((from_above[index], from_below[index])):
            for rank in range(NEED):
                place = pl.ds(pl.multiple_of(plan[2 * side + rank] * TILE, TILE), TILE)
                piece = slice(rank * TILE, (rank + 1) * TILE)
                key_ref[place, lanes] += returned[piece, :].astype(F32)
                piece = slice(PACK + rank * TILE, PACK + (rank + 1) * TILE)
                value_ref[place, lanes] += returned[piece, :].astype(F32)
        q_sum += jnp.sum(
            q_ref[:, lanes].astype(F32) * (q_gain_ref[:, lanes] * qg[index][...]),
            axis=1,
            keepdims=True,
        )
    grad_v_ref[...] = value_ref[...].astype(BF16)
    k_sum = jnp.sum(
        k_ref[...].astype(F32) * (k_gain_ref[...] * key_ref[...]), axis=1, keepdims=True
    )
    sums_ref[...] = to_rows([q_sum, k_sum])


def final_kernel(
    bounds, totals_ref, back_ref, q_ref, k_ref, q_gain_ref, k_gain_ref, key_ref, *refs
):
    count = len(bounds)
    qg, (grad_q_ref, grad_k_ref) = refs[:count], refs[count:]
    totals = to_columns(totals_ref[...], 4)
    back = to_columns(back_ref[...], 2)
    q_inverse = lax.rsqrt(totals[0] / FULL_WIDTH + NORM_EPS)
    k_inverse = lax.rsqrt(totals[2] / FULL_WIDTH + NORM_EPS)
    q_pull = q_inverse * q_inverse * q_inverse * (back[0] / FULL_WIDTH)
    k_pull = k_inverse * k_inverse * k_inverse * (back[1] / FULL_WIDTH)
    for index, (start, size) in enumerate(bounds):
        lanes = slice(start * HEAD_DIM, (start + size) * HEAD_DIM)
        grad_q_ref[:, lanes] = (
            q_inverse * (q_gain_ref[:, lanes] * qg[index][...])
            - q_ref[:, lanes].astype(F32) * q_pull
        ).astype(BF16)
    grad_k_ref[...] = (
        k_inverse * (k_gain_ref[...] * key_ref[...]) - k_ref[...].astype(F32) * k_pull
    ).astype(BF16)


def per_device(
    q_raw,
    k_raw,
    values,
    q_tangent,
    k_tangent,
    v_tangent,
    out_cotangent,
    q_gain,
    k_gain,
    tile_at_slot,
    key_tiles,
):
    rows, width = q_raw.shape
    head_count = width // HEAD_DIM
    tiles_here = rows // TILE
    devices = lax.axis_size("seq")
    bounds = chunk_bounds(head_count)
    position = lax.axis_index("seq").astype(jnp.int32).reshape(1)
    q_gain = q_gain.reshape(1, width)
    k_gain = k_gain.reshape(1, width)
    struct = jax.ShapeDtypeStruct

    plan, v_up, v_down = pl.pallas_call(
        functools.partial(prepare_kernel, devices, tiles_here),
        out_shape=[
            struct((16,), jnp.int32),
            struct((2 * PACK, width), BF16),
            struct((2 * PACK, width), BF16),
        ],
        in_specs=[SMEM] * 3 + [HBM] * 2,
        out_specs=[SMEM] + [HBM] * 2,
        scratch_shapes=[
            pltpu.SMEM((devices * tiles_here,), jnp.int32),
            pltpu.SemaphoreType.DMA((4 * NEED,)),
        ],
        compiler_params=params(),
        name="prepare",
    )(position, tile_at_slot, key_tiles, values, v_tangent)
    v_below = shifted(v_up, "seq", 1)
    v_above = shifted(v_down, "seq", -1)
    sums = pl.pallas_call(
        sums_kernel,
        out_shape=struct((8, rows), F32),
        in_specs=[VMEM] * 4,
        out_specs=VMEM,
        compiler_params=params(),
        name="sums",
    )(q_raw, k_raw, q_tangent, k_tangent)
    totals = head_total(sums, 0)
    packet_shapes = [
        struct((2 * PACK, size * HEAD_DIM), BF16) for _, size in bounds for _ in range(2)
    ]
    qn, qnt, kn, knt, *packets = pl.pallas_call(
        functools.partial(norm_kernel, bounds),
        out_shape=[struct((rows, width), BF16)] * 4 + packet_shapes,
        in_specs=[SMEM] + [VMEM] * 7,
        out_specs=[VMEM] * (4 + len(packet_shapes)),
        compiler_params=params(),
        name="norm",
    )(plan, totals, q_raw, k_raw, q_tangent, k_tangent, q_gain, k_gain)
    k_below = [shifted(packet, "seq", 1) for packet in packets[0::2]]
    k_above = [shifted(packet, "seq", -1) for packet in packets[1::2]]

    results = []
    for index, (start, size) in enumerate(bounds):
        def whole(head, plan_ref, start=start):
            return (0, start + head)

        def part(head, plan_ref):
            return (0, head)

        full_spec = pl.BlockSpec((rows, HEAD_DIM), whole)
        results.append(
            pl.pallas_call(
                functools.partial(attend_kernel, tiles_here),
                grid_spec=pltpu.PrefetchScalarGridSpec(
                    num_scalar_prefetch=1,
                    grid=(size,),
                    in_specs=[full_spec] * 7
                    + [pl.BlockSpec((2 * PACK, HEAD_DIM), part)] * 2
                    + [pl.BlockSpec((2 * PACK, HEAD_DIM), whole)] * 2,
                    out_specs=[pl.BlockSpec((rows, HEAD_DIM), part)] * 3
                    + [pl.BlockSpec((2 * rows, HEAD_DIM), part)]
                    + [pl.BlockSpec((2 * PACK, HEAD_DIM), part)] * 2,
                    scratch_shapes=[
                        pltpu.VMEM((2 * PACK, 4 * HEAD_DIM), BF16),
                        pltpu.VMEM((2 * PACK, 2 * HEAD_DIM), F32),
                    ]
                    + [pltpu.VMEM((rows, KSEL * TILE), F32)] * 3
                    + [pltpu.VMEM((rows, KSEL * TILE), BF16)] * 3,
                ),
                out_shape=[
                    struct((rows, size * HEAD_DIM), BF16),
                    struct((rows, size * HEAD_DIM), BF16),
                    struct((rows, size * HEAD_DIM), F32),
                    struct((2 * rows, size * HEAD_DIM), BF16),
                    struct((2 * PACK, size * HEAD_DIM), BF16),
                    struct((2 * PACK, size * HEAD_DIM), BF16),
                ],
                cost_estimate=pl.CostEstimate(
                    flops=20 * size * rows * KSEL * TILE * HEAD_DIM,
                    bytes_accessed=24 * size * rows * HEAD_DIM,
                    transcendentals=size * rows * KSEL * TILE,
                ),
                compiler_params=params(),
                name="attend",
            )(
                plan, qn, qnt, out_cotangent, kn, knt, values, v_tangent,
                k_below[index], k_above[index], v_below, v_above,
            )
        )
    outs, tangents, query_grads, locals_, to_below, to_above = zip(*results)
    from_above = [shifted(packet, "seq", -1) for packet in to_below]
    from_below = [shifted(packet, "seq", 1) for packet in to_above]
    count = len(bounds)
    grad_v, key_total, back_sums = pl.pallas_call(
        functools.partial(merge_kernel, bounds),
        out_shape=[
            struct((rows, width), BF16), struct((rows, width), F32), struct((8, rows), F32)
        ],
        in_specs=[SMEM] + [VMEM] * (4 + 4 * count),
        out_specs=[VMEM] * 3,
        scratch_shapes=[pltpu.VMEM((rows, width), F32)],
        compiler_params=params(),
        name="merge",
    )(plan, q_raw, k_raw, q_gain, k_gain, *query_grads, *locals_, *from_above, *from_below)
    back = head_total(back_sums, 1)
    grad_q, grad_k = pl.pallas_call(
        functools.partial(final_kernel, bounds),
        out_shape=[struct((rows, width), BF16)] * 2,
        in_specs=[VMEM] * (7 + count),
        out_specs=[VMEM] * 2,
        compiler_params=params(),
        name="final",
    )(totals, back, q_raw, k_raw, q_gain, k_gain, key_total, *query_grads)
    return (
        jnp.concatenate(outs, axis=1),
        jnp.concatenate(tangents, axis=1),
        grad_q,
        grad_k,
        grad_v,
    )


def solution(mesh):
    rows, lanes, copied = P("seq", "head"), P("head"), P()
    return jax.shard_map(
        per_device,
        mesh=mesh,
        in_specs=(rows,) * 7 + (lanes,) * 2 + (copied,) * 2,
        out_specs=(rows,) * 5,
        check_vma=False,
    )
```

```python
import functools

import jax
import jax.numpy as jnp
from jax import lax
from jax.experimental import pallas as pl
from jax.experimental.pallas import tpu as pltpu
from jax.sharding import PartitionSpec as P

HEADS = 20
HEAD_DIM = 128
TILE = 128
NEED = 2
KSEL = 6
FULL_WIDTH = HEADS * HEAD_DIM
NORM_EPS = 1e-06
SCALE = HEAD_DIM ** (-0.5)
PACK = NEED * TILE
VMEM_BYTES = 24 * 1024 * 1024
CHUNKS = (2, 3)

VMEM = pl.BlockSpec(memory_space=pltpu.VMEM)
SMEM = pl.BlockSpec(memory_space=pltpu.SMEM)
HBM = pl.BlockSpec(memory_space=pl.ANY)
F32 = jnp.float32
BF16 = jnp.bfloat16


def params():
    return pltpu.CompilerParams(vmem_limit_bytes=VMEM_BYTES)


def shifted(value, axis, steps):
    count = lax.axis_size(axis)
    leading, last = (max(0, -steps), min(count, count - steps))
    return lax.ppermute(value, axis, [(source, source + steps) for source in range(leading, last)])


def chunk_bounds(head_count):
    sizes = CHUNKS if sum(CHUNKS) == head_count else (1,) * head_count
    starts = [sum(sizes[:index]) for index in range(len(sizes))]
    return list(zip(starts, sizes))


def to_rows(columns):
    rows = columns[0].shape[0]
    lane = lax.broadcasted_iota(jnp.int32, (rows, 128), 1)
    packed = jnp.zeros((rows, 128), F32)
    for index, column in enumerate(columns):
        packed = jnp.where(lane == index, column, packed)
    return packed.T[:8]


def to_columns(rows, count):
    padded = jnp.concatenate([rows, jnp.zeros((120, rows.shape[1]), F32)], axis=0).T
    return [padded[:, index : index + 1] for index in range(count)]


def prepare_kernel(
    devices,
    tiles_here,
    position_ref,
    tile_at_slot,
    key_tiles,
    v_ref,
    vt_ref,
    plan_ref,
    up_ref,
    down_ref,
    slot_of,
    copy_sem,
):
    position = position_ref[0]

    def invert(slot, carry):
        slot_of[tile_at_slot[slot]] = slot
        return carry

    lax.fori_loop(0, devices * tiles_here, invert, 0)

    def remote_slots(device):
        return [
            slot_of[key_tiles[tile_at_slot[device * tiles_here + tile], column]]
            for tile in range(tiles_here)
            for column in range(tiles_here, KSEL)
        ]

    def first_last(slots, device):
        first = jnp.int32(tiles_here - 1)
        last = jnp.int32(0)
        for slot in slots:
            offset = slot - device * tiles_here
            inside = (offset >= 0) & (offset < tiles_here)
            first = jnp.where(inside, jnp.minimum(first, offset), first)
            last = jnp.where(inside, jnp.maximum(last, offset), last)
        return first, last

    above = remote_slots(jnp.minimum(position + 1, devices - 1))
    below = remote_slots(jnp.maximum(position - 1, 0))
    here = remote_slots(position)
    up_order = first_last(above, position)
    down_order = first_last(below, position)
    from_below, _ = first_last(here, position - 1)
    from_above, _ = first_last(here, position + 1)
    plan_ref[0], plan_ref[1] = up_order
    plan_ref[2], plan_ref[3] = down_order
    for index, slot in enumerate(here):
        low = jnp.where(slot == (position - 1) * tiles_here + from_below, 0, 1)
        high = jnp.where(slot == (position + 1) * tiles_here + from_above, 2, 3)
        plan_ref[4 + index] = jnp.where(slot < position * tiles_here, low, high)
    copies = []
    for order, packet in ((up_order, up_ref), (down_order, down_ref)):
        for rank in range(NEED):
            source = pl.ds(pl.multiple_of(order[rank] * TILE, TILE), TILE)
            for base, array_ref in ((0, v_ref), (PACK, vt_ref)):
                copies.append(
                    pltpu.make_async_copy(
                        array_ref.at[source, :],
                        packet.at[pl.ds(base + rank * TILE, TILE), :],
                        copy_sem.at[len(copies)],
                    )
                )
    for copy in copies:
        copy.start()
    for copy in copies:
        copy.wait()


def sums_kernel(q_ref, k_ref, qt_ref, kt_ref, sums_ref):
    columns = []
    for raw_ref, moving_ref in ((q_ref, qt_ref), (k_ref, kt_ref)):
        raw = raw_ref[...].astype(F32)
        moving = moving_ref[...].astype(F32)
        columns.append(jnp.sum(raw * raw, axis=1, keepdims=True))
        columns.append(jnp.sum(raw * moving, axis=1, keepdims=True))
    sums_ref[...] = to_rows(columns)


def exchange_kernel(count, part_ref, total_ref, arrived, send_sem, recv_sem):
    me = lax.axis_index("head")
    barrier = pltpu.get_barrier_semaphore()
    for step in range(1, count):
        pl.semaphore_signal(
            barrier,
            inc=1,
            device_id={"head": lax.rem(me + step, count)},
            device_id_type=pl.DeviceIdType.MESH,
        )
    pl.semaphore_wait(barrier, count - 1)
    copies = [
        pltpu.make_async_remote_copy(
            src_ref=part_ref,
            dst_ref=arrived.at[step - 1],
            send_sem=send_sem.at[step - 1],
            recv_sem=recv_sem.at[step - 1],
            device_id={"head": lax.rem(me + step, count)},
            device_id_type=pl.DeviceIdType.MESH,
        )
        for step in range(1, count)
    ]
    for copy in copies:
        copy.start()
    for copy in copies:
        copy.wait()
    total = part_ref[...]
    for step in range(1, count):
        total += arrived[step - 1]
    total_ref[...] = total


def head_total(part, collective_id):
    count = lax.axis_size("head")
    return pl.pallas_call(
        functools.partial(exchange_kernel, count),
        out_shape=jax.ShapeDtypeStruct(part.shape, F32),
        in_specs=[VMEM],
        out_specs=VMEM,
        scratch_shapes=[
            pltpu.VMEM((count - 1,) + part.shape, F32),
            pltpu.SemaphoreType.DMA((count - 1,)),
            pltpu.SemaphoreType.DMA((count - 1,)),
        ],
        compiler_params=pltpu.CompilerParams(
            collective_id=collective_id,
            has_side_effects=True,
            vmem_limit_bytes=2 * 1024 * 1024,
        ),
        name="exchange",
    )(part)


def norm_kernel(
    bounds,
    plan,
    totals_ref,
    q_ref,
    k_ref,
    qt_ref,
    kt_ref,
    q_gain_ref,
    k_gain_ref,
    qn_ref,
    qnt_ref,
    kn_ref,
    knt_ref,
    *packets,
):
    totals = to_columns(totals_ref[...], 4)
    for first, raw_ref, moving_ref, gain_ref, normed_ref, tangent_ref in (
        (2, k_ref, kt_ref, k_gain_ref, kn_ref, knt_ref),
        (0, q_ref, qt_ref, q_gain_ref, qn_ref, qnt_ref),
    ):
        inverse = lax.rsqrt(totals[first] / FULL_WIDTH + NORM_EPS)
        drift = totals[first + 1] / FULL_WIDTH
        raw = raw_ref[...].astype(F32)
        moving = moving_ref[...].astype(F32)
        gain = gain_ref[...]
        normed_ref[...] = (raw * inverse * gain).astype(BF16)
        tangent_ref[...] = (
            gain * (moving * inverse - raw * (inverse * inverse * inverse * drift))
        ).astype(BF16)
    for index, (start, size) in enumerate(bounds):
        lanes = slice(start * HEAD_DIM, (start + size) * HEAD_DIM)
        for side in range(2):
            packet = packets[2 * index + side]
            for rank in range(NEED):
                source = pl.ds(pl.multiple_of(plan[2 * side + rank] * TILE, TILE), TILE)
                packet[rank * TILE : (rank + 1) * TILE, :] = kn_ref[source, lanes]
                packet[PACK + rank * TILE : PACK + (rank + 1) * TILE, :] = knt_ref[source, lanes]


def dot(left, right, left_axis, right_axis):
    return lax.dot_general(
        left, right, (((left_axis,), (right_axis,)), ((), ())), preferred_element_type=F32
    )


def attend_kernel(
    tiles_here,
    plan,
    q_ref,
    qt_ref,
    co_ref,
    k_ref,
    kt_ref,
    v_ref,
    vt_ref,
    kb_ref,
    ka_ref,
    vb_ref,
    va_ref,
    out_ref,
    ot_ref,
    qg_ref,
    local_ref,
    below_ref,
    above_ref,
    remote,
    remote_sum,
    prob_buf,
    tangent_buf,
    grad_buf,
    probs_half,
    prob_tangent,
    score_grad,
):
    rows = tiles_here * TILE
    for base, kp_ref, vp_ref in ((0, kb_ref, vb_ref), (PACK, ka_ref, va_ref)):
        remote[base : base + PACK, 0:128] = kp_ref[:PACK, :]
        remote[base : base + PACK, 128:256] = kp_ref[PACK:, :]
        remote[base : base + PACK, 256:384] = vp_ref[:PACK, :]
        remote[base : base + PACK, 384:512] = vp_ref[PACK:, :]
    remote_sum[...] = jnp.zeros_like(remote_sum)
    tiles = [slice(tile * TILE, (tile + 1) * TILE) for tile in range(tiles_here)]
    places = [
        [
            pl.ds(pl.multiple_of(plan[4 + tile * 2 + column] * TILE, TILE), TILE)
            for column in range(2)
        ]
        for tile in range(tiles_here)
    ]

    def far(tile, start, stop):
        return jnp.concatenate([remote[place, start:stop] for place in places[tile]], axis=0)

    k_local = jnp.concatenate([k_ref[...], kt_ref[...]], axis=1)
    v_local = jnp.concatenate([v_ref[...], vt_ref[...]], axis=1)
    query, cotangent = q_ref[...], co_ref[...]
    moving = jnp.concatenate([qt_ref[...], query], axis=1)
    prob_buf[:, :rows] = dot(query, k_ref[...], 1, 1)
    tangent_buf[:, :rows] = dot(moving, k_local, 1, 1)
    grad_buf[:, :rows] = dot(cotangent, v_ref[...], 1, 1)
    for tile, here in enumerate(tiles):
        prob_buf[here, rows:] = dot(query[here], far(tile, 0, 128), 1, 1)
        tangent_buf[here, rows:] = dot(moving[here], far(tile, 0, 256), 1, 1)
        grad_buf[here, rows:] = dot(cotangent[here], far(tile, 256, 384), 1, 1)
    for here in tiles:
        scores = prob_buf[here, :]
        highest = jnp.max(scores, axis=1, keepdims=True)
        weights = jnp.exp((scores - highest) * SCALE)
        probs = weights * (1.0 / jnp.sum(weights, axis=1, keepdims=True))
        prob_buf[here, :] = probs
        probs_half[here, :] = probs.astype(BF16)
        score_tangent = tangent_buf[here, :] * SCALE
        centre = jnp.sum(probs * score_tangent, axis=1, keepdims=True)
        prob_tangent[here, :] = (probs * (score_tangent - centre)).astype(BF16)
    both = dot(probs_half[:, :rows], v_local, 1, 0)
    moved = dot(prob_tangent[:, :rows], v_ref[...], 1, 0)
    for tile, here in enumerate(tiles):
        pair = both[here] + dot(probs_half[here, rows:], far(tile, 256, 512), 1, 0)
        output = pair[:, :128].astype(BF16)
        out_ref[here, :] = output
        ot_ref[here, :] = (
            moved[here] + dot(prob_tangent[here, rows:], far(tile, 256, 384), 1, 0) + pair[:, 128:]
        ).astype(BF16)
        delta = jnp.sum(cotangent[here].astype(F32) * output.astype(F32), axis=1, keepdims=True)
        score_grad[here, :] = (prob_buf[here, :] * (grad_buf[here, :] - delta)).astype(BF16)
    near = dot(score_grad[:, :rows], k_ref[...], 1, 0)
    for tile, here in enumerate(tiles):
        qg_ref[here, :] = (near[here] + dot(score_grad[here, rows:], far(tile, 0, 128), 1, 0)) * SCALE
        key_grad = dot(score_grad[here, rows:], query[here], 0, 0)
        value_grad = dot(probs_half[here, rows:], cotangent[here], 0, 0)
        for column, place in enumerate(places[tile]):
            piece = slice(column * TILE, (column + 1) * TILE)
            remote_sum[place, :128] += key_grad[piece]
            remote_sum[place, 128:] += value_grad[piece]
    local_ref[:rows, :] = (dot(score_grad[:, :rows], query, 0, 0) * SCALE).astype(BF16)
    local_ref[rows:, :] = dot(probs_half[:, :rows], cotangent, 0, 0).astype(BF16)
    for base, part_ref in ((0, below_ref), (PACK, above_ref)):
        part_ref[:PACK, :] = (remote_sum[base : base + PACK, :128] * SCALE).astype(BF16)
        part_ref[PACK:, :] = remote_sum[base : base + PACK, 128:].astype(BF16)


def chained_attend_kernel(tiles_here, plan, *refs):
    attend_kernel(tiles_here, plan, *refs[:11], *refs[12:])


def merge_kernel(bounds, plan, q_ref, k_ref, q_gain_ref, k_gain_ref, *refs):
    count = len(bounds)
    qg, local, from_above, from_below = (refs[index * count : (index + 1) * count] for index in range(4))
    grad_v_ref, key_ref, sums_ref, value_ref = refs[4 * count :]
    rows = q_ref.shape[0]
    q_sum = jnp.zeros((rows, 1), F32)
    for index, (start, size) in enumerate(bounds):
        lanes = slice(start * HEAD_DIM, (start + size) * HEAD_DIM)
        key_ref[:, lanes] = local[index][:rows, :].astype(F32)
        value_ref[:, lanes] = local[index][rows:, :].astype(F32)
        for side, returned in enumerate((from_above[index], from_below[index])):
            for rank in range(NEED):
                place = pl.ds(pl.multiple_of(plan[2 * side + rank] * TILE, TILE), TILE)
                piece = slice(rank * TILE, (rank + 1) * TILE)
                key_ref[place, lanes] += returned[piece, :].astype(F32)
                piece = slice(PACK + rank * TILE, PACK + (rank + 1) * TILE)
                value_ref[place, lanes] += returned[piece, :].astype(F32)
        q_sum += jnp.sum(
            q_ref[:, lanes].astype(F32) * (q_gain_ref[:, lanes] * qg[index][...]),
            axis=1,
            keepdims=True,
        )
    grad_v_ref[...] = value_ref[...].astype(BF16)
    k_sum = jnp.sum(
        k_ref[...].astype(F32) * (k_gain_ref[...] * key_ref[...]), axis=1, keepdims=True
    )
    sums_ref[...] = to_rows([q_sum, k_sum])


def final_kernel(
    bounds, totals_ref, back_ref, q_ref, k_ref, q_gain_ref, k_gain_ref, key_ref, *refs
):
    count = len(bounds)
    qg, (grad_q_ref, grad_k_ref) = refs[:count], refs[count:]
    totals = to_columns(totals_ref[...], 4)
    back = to_columns(back_ref[...], 2)
    q_inverse = lax.rsqrt(totals[0] / FULL_WIDTH + NORM_EPS)
    k_inverse = lax.rsqrt(totals[2] / FULL_WIDTH + NORM_EPS)
    q_pull = q_inverse * q_inverse * q_inverse * (back[0] / FULL_WIDTH)
    k_pull = k_inverse * k_inverse * k_inverse * (back[1] / FULL_WIDTH)
    for index, (start, size) in enumerate(bounds):
        lanes = slice(start * HEAD_DIM, (start + size) * HEAD_DIM)
        grad_q_ref[:, lanes] = (
            q_inverse * (q_gain_ref[:, lanes] * qg[index][...])
            - q_ref[:, lanes].astype(F32) * q_pull
        ).astype(BF16)
    grad_k_ref[...] = (
        k_inverse * (k_gain_ref[...] * key_ref[...]) - k_ref[...].astype(F32) * k_pull
    ).astype(BF16)


def per_device(
    q_raw,
    k_raw,
    values,
    q_tangent,
    k_tangent,
    v_tangent,
    out_cotangent,
    q_gain,
    k_gain,
    tile_at_slot,
    key_tiles,
):
    rows, width = q_raw.shape
    head_count = width // HEAD_DIM
    tiles_here = rows // TILE
    devices = lax.axis_size("seq")
    bounds = chunk_bounds(head_count)
    position = lax.axis_index("seq").astype(jnp.int32).reshape(1)
    q_gain = q_gain.reshape(1, width)
    k_gain = k_gain.reshape(1, width)
    struct = jax.ShapeDtypeStruct

    plan, v_up, v_down = pl.pallas_call(
        functools.partial(prepare_kernel, devices, tiles_here),
        out_shape=[
            struct((16,), jnp.int32),
            struct((2 * PACK, width), BF16),
            struct((2 * PACK, width), BF16),
        ],
        in_specs=[SMEM] * 3 + [HBM] * 2,
        out_specs=[SMEM] + [HBM] * 2,
        scratch_shapes=[
            pltpu.SMEM((devices * tiles_here,), jnp.int32),
            pltpu.SemaphoreType.DMA((4 * NEED,)),
        ],
        compiler_params=params(),
        name="prepare",
    )(position, tile_at_slot, key_tiles, values, v_tangent)
    v_below = shifted(v_up, "seq", 1)
    v_above = shifted(v_down, "seq", -1)
    sums = pl.pallas_call(
        sums_kernel,
        out_shape=struct((8, rows), F32),
        in_specs=[VMEM] * 4,
        out_specs=VMEM,
        compiler_params=params(),
        name="sums",
    )(q_raw, k_raw, q_tangent, k_tangent)
    totals = head_total(sums, 0)
    packet_shapes = [
        struct((2 * PACK, size * HEAD_DIM), BF16) for _, size in bounds for _ in range(2)
    ]
    qn, qnt, kn, knt, *packets = pl.pallas_call(
        functools.partial(norm_kernel, bounds),
        out_shape=[struct((rows, width), BF16)] * 4 + packet_shapes,
        in_specs=[SMEM] + [VMEM] * 7,
        out_specs=[VMEM] * (4 + len(packet_shapes)),
        compiler_params=params(),
        name="norm",
    )(plan, totals, q_raw, k_raw, q_tangent, k_tangent, q_gain, k_gain)
    k_below = [shifted(packet, "seq", 1) for packet in packets[0::2]]
    k_above = [shifted(packet, "seq", -1) for packet in packets[1::2]]

    results = []
    for index, (start, size) in enumerate(bounds):
        def whole(head, plan_ref, start=start):
            return (0, start + head)

        def part(head, plan_ref):
            return (0, head)

        full_spec = pl.BlockSpec((rows, HEAD_DIM), whole)
        earlier = [results[-1][4]] if results else []
        body = chained_attend_kernel if results else attend_kernel
        results.append(
            pl.pallas_call(
                functools.partial(body, tiles_here),
                grid_spec=pltpu.PrefetchScalarGridSpec(
                    num_scalar_prefetch=1,
                    grid=(size,),
                    in_specs=[full_spec] * 7
                    + [pl.BlockSpec((2 * PACK, HEAD_DIM), part)] * 2
                    + [pl.BlockSpec((2 * PACK, HEAD_DIM), whole)] * 2
                    + [HBM] * len(earlier),
                    out_specs=[pl.BlockSpec((rows, HEAD_DIM), part)] * 3
                    + [pl.BlockSpec((2 * rows, HEAD_DIM), part)]
                    + [pl.BlockSpec((2 * PACK, HEAD_DIM), part)] * 2,
                    scratch_shapes=[
                        pltpu.VMEM((2 * PACK, 4 * HEAD_DIM), BF16),
                        pltpu.VMEM((2 * PACK, 2 * HEAD_DIM), F32),
                    ]
                    + [pltpu.VMEM((rows, KSEL * TILE), F32)] * 3
                    + [pltpu.VMEM((rows, KSEL * TILE), BF16)] * 3,
                ),
                out_shape=[
                    struct((rows, size * HEAD_DIM), BF16),
                    struct((rows, size * HEAD_DIM), BF16),
                    struct((rows, size * HEAD_DIM), F32),
                    struct((2 * rows, size * HEAD_DIM), BF16),
                    struct((2 * PACK, size * HEAD_DIM), BF16),
                    struct((2 * PACK, size * HEAD_DIM), BF16),
                ],
                cost_estimate=pl.CostEstimate(
                    flops=20 * size * rows * KSEL * TILE * HEAD_DIM,
                    bytes_accessed=24 * size * rows * HEAD_DIM,
                    transcendentals=size * rows * KSEL * TILE,
                ),
                compiler_params=params(),
                name="attend",
            )(
                plan, qn, qnt, out_cotangent, kn, knt, values, v_tangent,
                k_below[index], k_above[index], v_below, v_above, *earlier,
            )
        )
    outs, tangents, query_grads, locals_, to_below, to_above = zip(*results)
    from_above = [shifted(packet, "seq", -1) for packet in to_below]
    from_below = [shifted(packet, "seq", 1) for packet in to_above]
    count = len(bounds)
    grad_v, key_total, back_sums = pl.pallas_call(
        functools.partial(merge_kernel, bounds),
        out_shape=[
            struct((rows, width), BF16), struct((rows, width), F32), struct((8, rows), F32)
        ],
        in_specs=[SMEM] + [VMEM] * (4 + 4 * count),
        out_specs=[VMEM] * 3,
        scratch_shapes=[pltpu.VMEM((rows, width), F32)],
        compiler_params=params(),
        name="merge",
    )(plan, q_raw, k_raw, q_gain, k_gain, *query_grads, *locals_, *from_above, *from_below)
    back = head_total(back_sums, 1)
    grad_q, grad_k = pl.pallas_call(
        functools.partial(final_kernel, bounds),
        out_shape=[struct((rows, width), BF16)] * 2,
        in_specs=[VMEM] * (7 + count),
        out_specs=[VMEM] * 2,
        compiler_params=params(),
        name="final",
    )(totals, back, q_raw, k_raw, q_gain, k_gain, key_total, *query_grads)
    return (
        jnp.concatenate(outs, axis=1),
        jnp.concatenate(tangents, axis=1),
        grad_q,
        grad_k,
        grad_v,
    )


def solution(mesh):
    rows, lanes, copied = P("seq", "head"), P("head"), P()
    return jax.shard_map(
        per_device,
        mesh=mesh,
        in_specs=(rows,) * 7 + (lanes,) * 2 + (copied,) * 2,
        out_specs=(rows,) * 5,
        check_vma=False,
    )
```
